256 devices in a mesh: pipe: 4 (over y), expert: 32 (over z, x), dp: 2 (over core).
Axes of the slice: x: 4, y: 4, z: 8, core: 2. Of those that a mesh axis runs over, the one named last changes fastest.
Arguments:
- tokens: bfloat16 [2, 4096, 2048], P(None, ('expert', 'dp')), may hold values from -6 to 6
- cotangent: bfloat16 [2, 4096, 2048], P(None, ('expert', 'dp')), may hold values from -6 to 6
- routes: int32 [4, 2, 4096, 2], P('pipe', None, ('expert', 'dp')), may hold values from 0 to 31, all different within a row; in each aligned block of 64 rows (0 to 63, 64 to 127, ..., all dimensions but the last counted through in order) at most 6 rows name the same one
- gates: float32 [4, 2, 4096, 2], P('pipe', None, ('expert', 'dp')), may hold values from 0.1 to 0.6
- norm_gain: float32 [4, 2048], P('pipe'), may hold values from 0.5 to 1.5
- w_gate: bfloat16 [4, 32, 2048, 768], P('pipe', 'expert'), may hold values from -0.125 to 0.125
- w_up: bfloat16 [4, 32, 2048, 768], P('pipe', 'expert'), may hold values from -0.125 to 0.125
- w_down: bfloat16 [4, 32, 768, 2048], P('pipe', 'expert'), may hold values from -0.21875 to 0.21875
- in_a: bfloat16 [4, 32, 2048, 32], P('pipe', 'expert'), may hold values from -0.125 to 0.125
- in_b: bfloat16 [4, 32, 2, 16, 768], P('pipe', 'expert'), may hold values from -1.5 to 1.5
- down_a: bfloat16 [4, 32, 768, 16], P('pipe', 'expert'), may hold values from -0.21875 to 0.21875
- down_b: bfloat16 [4, 32, 16, 2048], P('pipe', 'expert'), may hold values from -1.5 to 1.5
Outputs:
- hidden: bfloat16 [4, 2, 4096, 2048], P('pipe', None, ('expert', 'dp'))
- input_grads: bfloat16 [4, 2, 4096, 2048], P('pipe', None, ('expert', 'dp'))
- grad_in_a: float32 [4, 32, 2048, 32], P('pipe', 'expert')
- grad_in_b: float32 [4, 32, 2, 16, 768], P('pipe', 'expert')
- grad_down_a: float32 [4, 32, 768, 16], P('pipe', 'expert')
- grad_down_b: float32 [4, 32, 16, 2048], P('pipe', 'expert')
The draws below stay inside these ranges and needn't reach their ends.
Inputs may be any that keep to these rules, and one draw needn't show every extreme that they name: `routes`: each token names 2 different experts; among the 64 tokens of one device's block (one section, one micro-batch, tokens b * 64 to (b + 1) * 64 - 1), no expert is named by more than 6 tokens.
All inputs are finite; a program needn't handle non-finite values.
Results may differ from the reference program's by a relative error of at most 0.039.
Values may be sent and summed in bfloat16 or wider, within the bound.
No kernel may reach another device: no remote copies, remote signals or barrier semaphores. Data moves between devices by JAX's collectives and lax.ppermute only.
A program may use at most 128 MiB of HBM per device.

```python
import math
import jax
import jax.numpy as jnp
import numpy as np
from jax import lax

D = 2048
FF = 768
RANK = 16
TOPK = 2
MICRO = 2
MB_TOK = 64
SECTIONS = 4
EXPERTS = 32
BLOCKS = 64
TOKENS = 4096
CAP = 6


def block_scale(stream_key, shape, cuts, low, high):
    factor_of, own = 1.0, jax.random.fold_in(stream_key, 6)
    for dim, shards_of in cuts:
        draws = jnp.exp(jax.random.uniform(jax.random.fold_in(own, dim), (shards_of,), jnp.float32, low / len(cuts), high / len(cuts)))
        factor_of = factor_of * jnp.repeat(draws, shape[dim] // shards_of).reshape([-1 if axis == dim else 1 for axis in range(len(shape))])
    return factor_of


def routed_block(stream_key, own, number, rows, count, top, bound, lean):
    sequence = jax.random.permutation(stream_key, count)
    heavy_load, ordinary = portions_of(count, rows * top, bound, lean, True), portions_of(count, rows * top, bound, lean, False)
    places = jnp.arange(count)

    def named(sizes, offset_by):
        used = int((sizes > 0).sum())
        fixed = max(1, used // 4)
        passed = fixed + (places - fixed + offset_by * (used - fixed)) % max(1, count - fixed)
        return jnp.zeros((count,), jnp.int32).at[sequence[jnp.where(places < fixed, places, passed)]].set(jnp.asarray(sizes, jnp.int32))

    sizes = jnp.where(number % 4 == 0, named(heavy_load, number // 4), named(ordinary, number - number // 4 - 1))
    mixed = jax.random.permutation(jax.random.fold_in(own, 3), count)
    giver, taker = mixed[0:count // 2 * 2:2], mixed[1:count // 2 * 2:2]
    margin = jnp.minimum(sizes[giver] - 1, bound - sizes[taker]) // 2
    margin = jnp.where((giver == sequence[0]) | (taker == sequence[0]) | (sizes[taker] == 0), 0, jnp.maximum(margin, 0))
    passed = jax.random.randint(jax.random.fold_in(own, 4), (count // 2,), 0, 1 << 20) % (margin + 1)
    sizes = sizes.at[giver].add(-passed).at[taker].add(passed)
    members = jnp.searchsorted(jnp.cumsum(sizes), jnp.arange(rows * top), side="right").astype(jnp.int32)
    listing = members.reshape(top, rows).T
    listing = listing[jax.random.permutation(jax.random.fold_in(own, 1), rows)]
    offset_by = jax.random.randint(jax.random.fold_in(own, 2), (rows, 1), 0, top)
    return jnp.take_along_axis(listing, (jnp.arange(top)[None, :] + offset_by) % top, axis=1)


def portions_of(amount, total, most, slope, full):
    portions = [(1 << 20) // math.isqrt(grade ** slope) + 1 for grade in range(1, amount + 1)]
    largest = most if full else min(most, max(-(-total // amount), total * portions[0] // sum(portions)))
    least = 1 if total - largest >= amount - 1 else 0
    counts, spare = [largest] + [least] * (amount - 1), total - largest - least * (amount - 1)
    while spare > 0:
        free = [i for i in range(1, amount) if counts[i] < largest] or [i for i in range(1, amount) if counts[i] < most]
        mass, remaining = sum([portions[i] for i in free]), spare
        for i in free:
            addition = min(most - counts[i], max(1, remaining * portions[i] // mass), spare)
            counts[i] = counts[i] + addition
            spare = spare - addition
    return np.array(counts)


def normal_values(rng, extent, width, reach, cuts=(), held_as=jnp.bfloat16):
    result = width * jax.random.normal(rng, extent, jnp.float32)
    if cuts:
        result = result * block_scale(rng, extent, cuts, -0.22, 0.18)
    return jnp.clip(result, -reach, reach).astype(held_as)


def setup_inputs(seed: int = 0) -> dict:
    splits = jax.random.split(jax.random.key(seed), 13)
    tokens = normal_values(splits[0], (MICRO, TOKENS, D), 1.0, 6.0, ((1, 64),))
    cotangent = normal_values(splits[1], (MICRO, TOKENS, D), 1.0, 6.0, ((1, 64),))
    routes_keys = jax.random.split(jax.random.fold_in(splits[2], 1), SECTIONS * MICRO * TOKENS // MB_TOK)
    routes_turns = jax.random.permutation(jax.random.fold_in(splits[2], 3), SECTIONS * MICRO * TOKENS // MB_TOK)
    routes = jax.vmap(lambda own, number: routed_block(jax.random.fold_in(splits[2], 2), own, number, MB_TOK, EXPERTS, TOPK, CAP, 1))(routes_keys, routes_turns).reshape((SECTIONS, MICRO, TOKENS, TOPK))
    gates = jnp.clip(jnp.exp(math.log(0.6) - 1.7917595 * jax.random.uniform(splits[3], (SECTIONS, MICRO, TOKENS, TOPK), jnp.float32) ** block_scale(splits[3], (SECTIONS, MICRO, TOKENS, TOPK), ((0, 4), (2, 64)), -0.2, 0.2)), 0.1, 0.6)
    norm_gain = jnp.clip(1.0 + 0.1 * jax.random.normal(splits[4], (SECTIONS, D), jnp.float32), 0.5, 1.5)
    w_gate = normal_values(splits[5], (SECTIONS, EXPERTS, D, FF), D ** -0.5, 0.125, ((0, 4), (1, 32)))
    w_up = normal_values(splits[6], (SECTIONS, EXPERTS, D, FF), D ** -0.5, 0.125, ((0, 4), (1, 32)))
    w_down = normal_values(splits[7], (SECTIONS, EXPERTS, FF, D), FF ** -0.5, 0.21875, ((0, 4), (1, 32)))
    in_a = normal_values(splits[8], (SECTIONS, EXPERTS, D, 2 * RANK), D ** -0.5, 0.125, ((0, 4), (1, 32)))
    in_b = normal_values(splits[9], (SECTIONS, EXPERTS, 2, RANK, FF), RANK ** -0.5, 1.5, ((0, 4), (1, 32)))
    down_a = normal_values(splits[10], (SECTIONS, EXPERTS, FF, RANK), FF ** -0.5, 0.21875, ((0, 4), (1, 32)))
    down_b = normal_values(splits[11], (SECTIONS, EXPERTS, RANK, D), RANK ** -0.5, 1.5, ((0, 4), (1, 32)))
    return {"tokens": tokens, "cotangent": cotangent, "routes": routes, "gates": gates, "norm_gain": norm_gain, "w_gate": w_gate, "w_up": w_up, "w_down": w_down, "in_a": in_a, "in_b": in_b, "down_a": down_a, "down_b": down_b}


EPS = 1e-06

def normalize(section_in, norm_scale):
    values = section_in.astype(jnp.float32)
    inverse = lax.rsqrt(lax.optimization_barrier(jnp.mean(values * values, axis=-1, keepdims=True)) + EPS)
    return ((values * inverse * norm_scale).astype(jnp.bfloat16), inverse)

def normalize_back(grad_norm, section_in, inverse, norm_scale):
    normed = section_in.astype(jnp.float32) * inverse
    scaled = grad_norm * norm_scale
    return inverse * (scaled - normed * lax.optimization_barrier(jnp.mean(scaled * normed, axis=-1, keepdims=True)))

def expert_forward(slot_rows, w_gate, w_up, w_down, in_a, in_b, down_a, down_b):
    low_rank = down_a.shape[1]
    low_in = jnp.dot(slot_rows, in_a, preferred_element_type=jnp.float32).astype(jnp.bfloat16)
    gate_pre = jnp.dot(slot_rows, w_gate, preferred_element_type=jnp.float32) + jnp.dot(low_in[:, :low_rank], in_b[0], preferred_element_type=jnp.float32)
    up_pre = jnp.dot(slot_rows, w_up, preferred_element_type=jnp.float32) + jnp.dot(low_in[:, low_rank:], in_b[1], preferred_element_type=jnp.float32)
    activated = (jax.nn.silu(gate_pre) * up_pre).astype(jnp.bfloat16)
    low_down = jnp.dot(activated, down_a, preferred_element_type=jnp.float32).astype(jnp.bfloat16)
    expert_out = (jnp.dot(activated, w_down, preferred_element_type=jnp.float32) + jnp.dot(low_down, down_b, preferred_element_type=jnp.float32)).astype(jnp.bfloat16)
    return (expert_out, (low_in, gate_pre, up_pre, activated, low_down))

def expert_backward(slot_rows, grad_out, saved_state, w_gate, w_up, w_down, in_a, in_b, down_a, down_b):
    low_in, gate_pre, up_pre, activated, low_down = saved_state
    low_rank = down_a.shape[1]
    grad_low_down = jnp.dot(grad_out, down_b.T, preferred_element_type=jnp.float32).astype(jnp.bfloat16)
    grad_down_b = jnp.dot(low_down.T, grad_out, preferred_element_type=jnp.float32)
    grad_down_a = jnp.dot(activated.T, grad_low_down, preferred_element_type=jnp.float32)
    grad_act = jnp.dot(grad_out, w_down.T, preferred_element_type=jnp.float32) + jnp.dot(grad_low_down, down_a.T, preferred_element_type=jnp.float32)
    sigmoid = jax.nn.sigmoid(gate_pre)
    grad_gate = (grad_act * up_pre * sigmoid * (1.0 + gate_pre * (1.0 - sigmoid))).astype(jnp.bfloat16)
    grad_up = (grad_act * gate_pre * sigmoid).astype(jnp.bfloat16)
    grad_in_b = jnp.stack([jnp.dot(low_in[:, :low_rank].T, grad_gate, preferred_element_type=jnp.float32), jnp.dot(low_in[:, low_rank:].T, grad_up, preferred_element_type=jnp.float32)])
    grad_low_in = jnp.concatenate([jnp.dot(grad_gate, in_b[0].T, preferred_element_type=jnp.float32), jnp.dot(grad_up, in_b[1].T, preferred_element_type=jnp.float32)], axis=1).astype(jnp.bfloat16)
    grad_in_a = jnp.dot(slot_rows.T, grad_low_in, preferred_element_type=jnp.float32)
    grad_rows = (jnp.dot(grad_gate, w_gate.T, preferred_element_type=jnp.float32) + jnp.dot(grad_up, w_up.T, preferred_element_type=jnp.float32) + jnp.dot(grad_low_in, in_a.T, preferred_element_type=jnp.float32)).astype(jnp.bfloat16)
    return (grad_rows, (grad_in_a, grad_in_b, grad_down_a, grad_down_b))

def section_tables(routes_micro):
    flat_routes = routes_micro.reshape(BLOCKS, MB_TOK * TOPK)
    onehot = (flat_routes[:, :, None] == jnp.arange(EXPERTS, dtype=jnp.int32)[None, None, :]).astype(jnp.int32)
    earlier = jnp.cumsum(onehot, axis=1) - onehot
    position = lax.optimization_barrier(jnp.sum(earlier * onehot, axis=2)).reshape(TOKENS, TOPK).astype(jnp.int32)
    owner_block = (jnp.arange(TOKENS, dtype=jnp.int32) // MB_TOK)[:, None]
    bucket_slot = (owner_block * CAP + position).astype(jnp.int32)
    source_token = jnp.broadcast_to(jnp.arange(TOKENS, dtype=jnp.int32)[:, None], (TOKENS, TOPK))
    bucket_table = jnp.full((EXPERTS, BLOCKS * CAP), TOKENS, dtype=jnp.int32)
    bucket_table = bucket_table.at[routes_micro.reshape(-1), bucket_slot.reshape(-1)].set(source_token.reshape(-1))
    return (bucket_table, bucket_slot)

def section_forward(section_in, routes_micro, gates_micro, layer):
    normed, inverse = normalize(section_in, layer[0])
    bucket_table, bucket_slot = section_tables(routes_micro)
    padded = jnp.concatenate([normed, jnp.zeros((1, D), normed.dtype)], axis=0)

    def one_expert(operands):
        slot_rows = padded[operands[0]]
        return expert_forward(slot_rows, operands[1], operands[2], operands[3], operands[4], operands[5], operands[6], operands[7])[0]
    expert_out = lax.map(one_expert, (bucket_table,) + tuple(layer[1:]))
    picked = expert_out[routes_micro, bucket_slot].astype(jnp.float32)
    mixed_out = section_in.astype(jnp.float32) + lax.optimization_barrier(jnp.sum(gates_micro[:, :, None] * picked, axis=1))
    return mixed_out.astype(jnp.bfloat16)

def section_backward(section_in, grad_next, routes_micro, gates_micro, layer):
    normed, inverse = normalize(section_in, layer[0])
    bucket_table, bucket_slot = section_tables(routes_micro)
    padded = jnp.concatenate([normed, jnp.zeros((1, D), normed.dtype)], axis=0)
    grad_slots = (gates_micro[:, :, None] * grad_next.astype(jnp.float32)[:, None, :]).astype(jnp.bfloat16)
    grad_table = jnp.zeros((EXPERTS, BLOCKS * CAP, D), grad_slots.dtype).at[routes_micro, bucket_slot].set(grad_slots)

    def one_expert(operands):
        slot_rows = padded[operands[0]]
        weights = operands[2:]
        expert_out, saved_state = expert_forward(slot_rows, weights[0], weights[1], weights[2], weights[3], weights[4], weights[5], weights[6])
        return expert_backward(slot_rows, operands[1], saved_state, weights[0], weights[1], weights[2], weights[3], weights[4], weights[5], weights[6])
    grad_rows, adapter_grads = lax.map(one_expert, (bucket_table, grad_table) + tuple(layer[1:]))
    grad_norm = lax.optimization_barrier(jnp.sum(grad_rows[routes_micro, bucket_slot].astype(jnp.float32), axis=1))
    grad_in = grad_next.astype(jnp.float32) + normalize_back(grad_norm, section_in, inverse, layer[0])
    return (grad_in.astype(jnp.bfloat16), adapter_grads)

def reference(tokens, cotangent, routes, gates, norm_gain, w_gate, w_up, w_down, in_a, in_b, down_a, down_b):
    current = [tokens[micro_index] for micro_index in range(MICRO)]
    section_inputs = []
    hidden = []
    for section_index in range(SECTIONS):
        layer = (norm_gain[section_index], w_gate[section_index], w_up[section_index], w_down[section_index], in_a[section_index], in_b[section_index], down_a[section_index], down_b[section_index])
        section_inputs.append(current)
        produced = []
        for micro_index in range(MICRO):
            produced.append(section_forward(current[micro_index], routes[section_index, micro_index], gates[section_index, micro_index], layer))
        current = produced
        hidden.append(jnp.stack(produced))
    grads_back = [cotangent[micro_index] for micro_index in range(MICRO)]
    input_grads = [None] * SECTIONS
    totals = [None] * SECTIONS
    for section_index in reversed(range(SECTIONS)):
        layer = (norm_gain[section_index], w_gate[section_index], w_up[section_index], w_down[section_index], in_a[section_index], in_b[section_index], down_a[section_index], down_b[section_index])
        produced = []
        summed = None
        for micro_index in range(MICRO):
            grad_in, adapter_grads = section_backward(section_inputs[section_index][micro_index], grads_back[micro_index], routes[section_index, micro_index], gates[section_index, micro_index], layer)
            produced.append(grad_in)
            if summed is None:
                summed = adapter_grads
            else:
                summed = tuple((summed[item] + adapter_grads[item] for item in range(4)))
        grads_back = produced
        input_grads[section_index] = jnp.stack(produced)
        totals[section_index] = summed
    return (jnp.stack(hidden), jnp.stack(input_grads), jnp.stack([totals[section_index][0] for section_index in range(SECTIONS)]), jnp.stack([totals[section_index][1] for section_index in range(SECTIONS)]), jnp.stack([totals[section_index][2] for section_index in range(SECTIONS)]), jnp.stack([totals[section_index][3] for section_index in range(SECTIONS)]))
```

```python
import functools

import jax
import jax.numpy as jnp
import numpy as np
from jax import lax
from jax.experimental import pallas as pl
from jax.experimental.pallas import tpu as pltpu
from jax.sharding import PartitionSpec as P

EPS = 1e-06
SLOTS = 6
LANES = 128
F32 = jnp.float32
BF16 = jnp.bfloat16


def dot(left, right):
    return jnp.dot(left, right, preferred_element_type=F32)


def dot_nt(left, right):
    return lax.dot_general(left, right, (((1,), (1,)), ((), ())), preferred_element_type=F32)


def dot_tn(left, right):
    return lax.dot_general(left, right, (((0,), (0,)), ((), ())), preferred_element_type=F32)


def pack(read, out_ref, wide, peers, chunks):
    stride = SLOTS * chunks
    for slot in range(SLOTS):
        for chunk in range(chunks):
            wide[pl.ds(slot * chunks + chunk, peers, stride=stride), :] = read(slot, chunk)
    for peer in range(peers):
        out_ref[peer] = wide[peer * stride : (peer + 1) * stride, :].astype(BF16)


def unpack(in_ref, rows, wide, peers, chunks):
    stride = SLOTS * chunks
    for peer in range(peers):
        wide[peer * stride : (peer + 1) * stride, :] = in_ref[peer].astype(F32)
    for slot in range(SLOTS):
        for chunk in range(chunks):
            rows[slot * peers : (slot + 1) * peers, chunk * LANES : (chunk + 1) * LANES] = wide[
                pl.ds(slot * chunks + chunk, peers, stride=stride), :
            ].astype(BF16)


def tables_kernel(peers, routes, routes_t, gates, gates_t, place, scale_hi, scale_lo, pick, mix_hi, mix_lo):
    micros, rows, _ = routes.shape
    slots = SLOTS * peers
    assert peers & (peers - 1) == 0
    shift = peers.bit_length() - 1
    for micro in range(micros):
        number = lax.broadcasted_iota(jnp.int32, (slots, rows), 0)
        expert, position = number & (peers - 1), (number >> shift).astype(F32)
        first = routes_t[micro, 0:1, :] == expert
        second = routes_t[micro, 1:2, :] == expert
        named = jnp.where(first | second, 1.0, 0.0)
        earlier = lax.broadcasted_iota(jnp.int32, (rows, rows), 0) < lax.broadcasted_iota(
            jnp.int32, (rows, rows), 1
        )
        before = dot(named.astype(BF16), jnp.where(earlier, 1.0, 0.0).astype(BF16))
        chosen = jnp.where(before == position, named, 0.0)
        weight = jnp.where(first, gates_t[micro, 0:1, :], 0.0) + jnp.where(
            second, gates_t[micro, 1:2, :], 0.0
        )
        weight = weight * chosen
        high = weight.astype(BF16)
        place[micro] = chosen.astype(BF16)
        scale_hi[micro] = high
        scale_lo[micro] = (weight - high.astype(F32)).astype(BF16)

        number = lax.broadcasted_iota(jnp.int32, (rows, slots), 1)
        expert, position = number & (peers - 1), (number >> shift).astype(F32)
        first = routes[micro, :, 0:1] == expert
        second = routes[micro, :, 1:2] == expert
        named = jnp.where(first | second, 1.0, 0.0)
        earlier = lax.broadcasted_iota(jnp.int32, (rows, rows), 1) < lax.broadcasted_iota(
            jnp.int32, (rows, rows), 0
        )
        before = dot(jnp.where(earlier, 1.0, 0.0).astype(BF16), named.astype(BF16))
        chosen = jnp.where(before == position, named, 0.0)
        weight = jnp.where(first, gates[micro, :, 0:1], 0.0) + jnp.where(
            second, gates[micro, :, 1:2], 0.0
        )
        weight = weight * chosen
        high = weight.astype(BF16)
        pick[micro] = chosen.astype(BF16)
        mix_hi[micro] = high
        mix_lo[micro] = (weight - high.astype(F32)).astype(BF16)


def choose(refs, which):
    value = refs[0][...]
    for index in range(1, len(refs)):
        value = jnp.where(which == index, refs[index][...], value)
    return value


def dispatch_kernel(dims, kinds, source_count, flags, *refs):
    peers, chunks, base = dims
    sources = refs[:source_count]
    gain, place, scale_hi, scale_lo = refs[source_count : source_count + 4]
    out_ref = refs[source_count + 4]
    wide, rows = refs[-2:]
    is_forward, micro = flags[base], flags[base + 1]
    current = choose(sources, flags[base + 2])
    if source_count > 1:
        refs[source_count + 5][...] = current

    def forward():
        values = current.astype(F32)
        inverse = lax.rsqrt(jnp.mean(values * values, axis=-1, keepdims=True) + EPS)
        rows[...] = dot(place[micro], (values * inverse * gain[...]).astype(BF16))

    def backward():
        rows[...] = dot(scale_hi[micro], current) + dot(scale_lo[micro], current)

    if kinds == "F":
        forward()
    elif kinds == "B":
        backward()
    else:
        pl.when(is_forward == 1)(forward)
        pl.when(is_forward == 0)(backward)
    pack(
        lambda slot, chunk: rows[
            slot * peers : (slot + 1) * peers, chunk * LANES : (chunk + 1) * LANES
        ],
        out_ref,
        wide,
        peers,
        chunks,
    )


def combine_kernel(dims, kinds, section_count, grad_count, flags, *refs):
    peers, chunks, base = dims
    returned = refs[0]
    sections = refs[1 : 1 + section_count]
    grads = refs[1 + section_count : 1 + section_count + grad_count]
    gain, pick, mix_hi, mix_lo, out_ref, wide, rows = refs[1 + section_count + grad_count :]
    is_forward, micro = flags[base], flags[base + 1]
    unpack(returned, rows, wide, peers, chunks)

    def forward():
        mixed = dot(mix_hi[micro], rows[...]) + dot(mix_lo[micro], rows[...])
        out_ref[...] = (choose(sections, flags[base + 2]).astype(F32) + mixed).astype(BF16)

    def backward():
        section_in = choose(sections, flags[base + 2]).astype(F32)
        grad_next = choose(grads, flags[base + 3]).astype(F32)
        inverse = lax.rsqrt(jnp.mean(section_in * section_in, axis=-1, keepdims=True) + EPS)
        scaled = dot(pick[micro], rows[...]) * gain[...]
        normed = section_in * inverse
        shared = jnp.mean(scaled * normed, axis=-1, keepdims=True)
        out_ref[...] = (grad_next + inverse * (scaled - normed * shared)).astype(BF16)

    if kinds == "F":
        forward()
    elif kinds == "B":
        backward()
    else:
        pl.when(is_forward == 1)(forward)
        pl.when(is_forward == 0)(backward)


def forward_kernel(dims, has_store, received, w_gate, w_up, w_down, in_a, in_b, down_a, down_b, *refs):
    peers, chunks, low_rank = dims
    sent, rows, low_in, gate_pre, up_pre, wide, total, low_total = refs[4 * has_store :]
    step = pl.program_id(0)

    @pl.when(step == 0)
    def _():
        unpack(received, rows.at[0], wide, peers, chunks)
        low_in[0] = dot_nt(rows[0], in_a[...]).astype(BF16)

    slot_rows, low = rows[0], low_in[0]
    gate = dot(slot_rows, w_gate[...]) + dot(low[:, :low_rank], in_b[0])
    up = dot(slot_rows, w_up[...]) + dot(low[:, low_rank:], in_b[1])
    gate_pre[0] = gate
    up_pre[0] = up
    activated = (gate * jax.nn.sigmoid(gate) * up).astype(BF16)
    low_part = dot_nt(activated, down_a[...])
    part = dot(activated, w_down[...])

    @pl.when(step == 0)
    def _():
        total[...] = part
        low_total[...] = low_part

    @pl.when(step > 0)
    def _():
        total[...] += part
        low_total[...] += low_part

    @pl.when(step == pl.num_programs(0) - 1)
    def _():
        total[...] += dot(low_total[...].astype(BF16), down_b[...])
        pack(
            lambda slot, chunk: total[
                slot * peers : (slot + 1) * peers, chunk * LANES : (chunk + 1) * LANES
            ],
            sent,
            wide,
            peers,
            chunks,
        )


def backward_kernel(dims, received_count, has_other, flags, *refs):
    peers, chunks, low_rank, base = dims
    received = refs[:received_count]
    other = refs[received_count]
    refs = refs[received_count + has_other :]
    (rows, low_in, gate_pre, up_pre, w_gate, w_up, w_down, in_a, in_b, down_a, down_b) = refs[:11]
    (sent, grad_in_a, grad_in_b, grad_down_a, grad_down_b) = refs[11:16]
    (wide, grad_out, grad_low_down, total, low_total, grad_low_in) = refs[16:]
    step = pl.program_id(0)
    last = step == pl.num_programs(0) - 1
    active = flags[base] == 1

    @pl.when(active)
    def _():
        @pl.when(step == 0)
        def _():
            if received_count == 1:
                unpack(received[0], grad_out, wide, peers, chunks)
            else:
                for index in range(received_count):

                    @pl.when(flags[base + 2] == index)
                    def _():
                        unpack(received[index], grad_out, wide, peers, chunks)

            grad_low_down[...] = dot_nt(grad_out[...], down_b[...]).astype(BF16)

        low = low_in[0]
        gate, up = gate_pre[0], up_pre[0]
        sigmoid = jax.nn.sigmoid(gate)
        silu = gate * sigmoid
        activated = (silu * up).astype(BF16)
        grad_act = dot_nt(grad_out[...], w_down[...]) + dot(grad_low_down[...], down_a[...])
        grad_gate = (grad_act * up * sigmoid * (1.0 + gate * (1.0 - sigmoid))).astype(BF16)
        grad_up = (grad_act * silu).astype(BF16)
        grad_in_b[0] = dot_tn(low[:, :low_rank], grad_gate)
        grad_in_b[1] = dot_tn(low[:, low_rank:], grad_up)
        grad_down_a[...] = dot_tn(grad_low_down[...], activated)
        low_part = dot_nt(activated, down_a[...])
        in_part = jnp.concatenate([dot_nt(grad_gate, in_b[0]), dot_nt(grad_up, in_b[1])], axis=1)
        part = dot_nt(grad_gate, w_gate[...]) + dot_nt(grad_up, w_up[...])

        @pl.when(step == 0)
        def _():
            total[...] = part
            low_total[...] = low_part
            grad_low_in[...] = in_part

        @pl.when(step > 0)
        def _():
            total[...] += part
            low_total[...] += low_part
            grad_low_in[...] += in_part

        @pl.when(last)
        def _():
            low_grad = grad_low_in[...].astype(BF16)
            total[...] += dot(low_grad, in_a[...])
            pack(
                lambda slot, chunk: total[
                    slot * peers : (slot + 1) * peers, chunk * LANES : (chunk + 1) * LANES
                ],
                sent,
                wide,
                peers,
                chunks,
            )
            grad_in_a[...] = dot_tn(low_grad, rows[0])
            grad_down_b[...] = dot_tn(low_total[...].astype(BF16), grad_out[...])

    if has_other:

        @pl.when(jnp.logical_not(active) & last)
        def _():
            sent[...] = other[...]


def params(megabytes):
    return pltpu.CompilerParams(vmem_limit_bytes=megabytes * 1024 * 1024)


def whole(shape):
    zeros = (0,) * len(shape)
    return pl.BlockSpec(shape, lambda *_: zeros)


def rank_flags(sections, micros):
    assert sections == 4 and micros == 2
    last = sections - 1
    ticks = 2 * sections
    table = np.zeros((sections, ticks, 12), np.int32)
    for rank in range(sections):
        for tick in range(ticks):
            row = table[rank, tick]
            forward = tick - rank if tick - rank in (0, 1) else None
            backward = tick - (2 * last - rank)
            backward = backward if backward in (0, 1) else None
            if forward is not None:
                row[0:2] = 1, forward
            elif backward is not None:
                row[0:2] = 0, backward
            elif rank == last and tick < 2:
                row[0:2] = 0, tick
            if tick == 0:
                row[2] = 1 if rank == last else 0
            elif tick == 1:
                row[2] = 2 if rank == last else (0 if rank == 0 else 1)
            if backward is not None:
                row[4:6] = 1, rank + backward
                row[6] = 0 if rank == last else 1
                row[8:10] = 0, backward
            elif forward is not None:
                row[8:10] = 1, forward
            elif rank == last and tick in (5, 6):
                row[8:10] = 1, tick - 5
            if tick == 4:
                row[10:12] = (0, 0) if rank == last else (1, 1)
            elif tick == 5:
                row[10] = 1 if rank == 1 else 0
            elif tick == 6:
                row[10] = {1: 0, 0: 1, 3: 2}.get(rank, 0)
    return table.reshape(sections, -1)


def body(
    tokens, cotangent, routes, gates, norm_gain, w_gate, w_up, w_down, in_a, in_b, down_a, down_b
):
    section_index = lax.axis_index("pipe")
    sections = lax.axis_size("pipe")
    peers = lax.axis_size("expert")
    micros, tok_rows, model = tokens.shape
    hidden_width = w_gate.shape[3]
    low_rank = down_a.shape[3]
    slots = SLOTS * peers
    chunks = model // LANES
    ticks = 2 * sections
    forward_ticks = sections + micros - 1
    block = hidden_width // 3
    flags = lax.dynamic_index_in_dim(
        jnp.asarray(rank_flags(sections, micros)), section_index, 0, keepdims=False
    )
    w_gate, w_up, w_down = w_gate[0, 0], w_up[0, 0], w_down[0, 0]
    in_a, in_b, down_a, down_b = in_a[0, 0].T, in_b[0, 0], down_a[0, 0].T, down_b[0, 0]
    buffer = jax.ShapeDtypeStruct((peers, SLOTS * chunks, LANES), BF16)
    block_rows = jax.ShapeDtypeStruct((tok_rows, model), BF16)
    wide = pltpu.VMEM((peers * SLOTS * chunks, LANES), F32)

    routes, gates = routes[0], gates[0]
    table_in = jax.ShapeDtypeStruct((micros, slots, tok_rows), BF16)
    table_out = jax.ShapeDtypeStruct((micros, tok_rows, slots), BF16)
    place, scale_hi, scale_lo, pick, mix_hi, mix_lo = pl.pallas_call(
        functools.partial(tables_kernel, peers),
        out_shape=[table_in] * 3 + [table_out] * 3,
        name="tables",
    )(routes, routes.transpose(0, 2, 1), gates, gates.transpose(0, 2, 1))

    def exchange(rows):
        return lax.all_to_all(rows, "expert", split_axis=0, concat_axis=0, tiled=True)

    def dispatch(tick, kinds, sources):
        arrays = [source if source.ndim == 2 else source for source in sources]
        specs = [
            whole(source.shape)
            if source.ndim == 2
            else pl.BlockSpec((pl.squeezed,) + source.shape[1:], lambda *_, t=tick: (t, 0, 0))
            for source in sources
        ]
        single = len(sources) == 1
        operands = arrays + [norm_gain, place, scale_hi, scale_lo]
        specs += [whole(x.shape) for x in operands[len(arrays) :]]
        result = pl.pallas_call(
            functools.partial(dispatch_kernel, (peers, chunks, tick * 12), kinds, len(sources)),
            out_shape=[buffer] if single else [buffer, block_rows],
            grid_spec=pltpu.PrefetchScalarGridSpec(
                num_scalar_prefetch=1,
                grid=(1,),
                in_specs=specs,
                out_specs=[whole(buffer.shape)] + ([] if single else [whole(block_rows.shape)]),
                scratch_shapes=[wide, pltpu.VMEM((slots, model), F32)],
            ),
            compiler_params=params(24),
            name="dispatch",
        )(flags, *operands)
        return result[0], sources[0] if single else result[1]

    def combine(tick, kinds, returned, section_inputs, grads):
        operands = [returned] + list(section_inputs)
        specs = [whole(x.shape) for x in operands]
        for grad in grads:
            operands.append(grad)
            specs.append(
                whole(grad.shape)
                if grad.ndim == 2
                else pl.BlockSpec(
                    (pl.squeezed,) + grad.shape[1:], lambda *_, m=tick - 3: (m, 0, 0)
                )
            )
        more = [norm_gain, pick, mix_hi, mix_lo]
        return pl.pallas_call(
            functools.partial(
                combine_kernel,
                (peers, chunks, tick * 12 + 8),
                kinds,
                len(section_inputs),
                len(grads),
            ),
            out_shape=block_rows,
            grid_spec=pltpu.PrefetchScalarGridSpec(
                num_scalar_prefetch=1,
                grid=(1,),
                in_specs=specs + [whole(x.shape) for x in more],
                out_specs=whole(block_rows.shape),
                scratch_shapes=[wide, pltpu.VMEM((slots, model), BF16)],
            ),
            compiler_params=params(24),
            name="combine",
        )(flags, *operands, *more)

    weights = (w_gate, w_up, w_down, in_a, in_b, down_a, down_b)
    weight_specs = [
        pl.BlockSpec((model, block), lambda f, *_: (0, f)),
        pl.BlockSpec((model, block), lambda f, *_: (0, f)),
        pl.BlockSpec((block, model), lambda f, *_: (f, 0)),
        whole(in_a.shape),
        pl.BlockSpec((2, low_rank, block), lambda f, *_: (0, 0, f)),
        pl.BlockSpec((low_rank, block), lambda f, *_: (0, f)),
        whole(down_b.shape),
    ]
    state_shapes = [
        jax.ShapeDtypeStruct((forward_ticks, slots, model), BF16),
        jax.ShapeDtypeStruct((forward_ticks, slots, 2 * low_rank), BF16),
        jax.ShapeDtypeStruct((forward_ticks, slots, hidden_width), F32),
        jax.ShapeDtypeStruct((forward_ticks, slots, hidden_width), F32),
    ]

    def state_specs(slot_of):
        return [
            pl.BlockSpec((1, slots, model), lambda f, *s: (slot_of(s), 0, 0)),
            pl.BlockSpec((1, slots, 2 * low_rank), lambda f, *s: (slot_of(s), 0, 0)),
            pl.BlockSpec((1, slots, block), lambda f, *s: (slot_of(s), 0, f)),
            pl.BlockSpec((1, slots, block), lambda f, *s: (slot_of(s), 0, f)),
        ]

    def expert_forward(tick, received, state):
        has_store = state is not None
        result = pl.pallas_call(
            functools.partial(forward_kernel, (peers, chunks, low_rank), has_store),
            out_shape=[buffer] + state_shapes,
            grid=(hidden_width // block,),
            in_specs=[whole(buffer.shape)]
            + weight_specs
            + ([pl.BlockSpec(memory_space=pl.ANY)] * 4 if has_store else []),
            out_specs=[whole(buffer.shape)] + state_specs(lambda s: tick),
            scratch_shapes=[
                wide,
                pltpu.VMEM((slots, model), F32),
                pltpu.VMEM((slots, low_rank), F32),
            ],
            input_output_aliases={8: 1, 9: 2, 10: 3, 11: 4} if has_store else {},
            compiler_params=params(40),
            name="expert_forward",
        )(received, *weights, *(state if has_store else ()))
        return result[0], result[1:]

    def expert_backward(tick, received, other, state):
        base = tick * 12 + 4
        others = [] if other is None else [other]
        return pl.pallas_call(
            functools.partial(
                backward_kernel, (peers, chunks, low_rank, base), len(received), len(others)
            ),
            out_shape=[
                buffer,
                jax.ShapeDtypeStruct((2 * low_rank, model), F32),
                jax.ShapeDtypeStruct((2, low_rank, hidden_width), F32),
                jax.ShapeDtypeStruct((low_rank, hidden_width), F32),
                jax.ShapeDtypeStruct((low_rank, model), F32),
            ],
            grid_spec=pltpu.PrefetchScalarGridSpec(
                num_scalar_prefetch=1,
                grid=(hidden_width // block,),
                in_specs=[whole(buffer.shape)] * (len(received) + len(others))
                + state_specs(lambda s: s[0][base + 1])
                + weight_specs,
                out_specs=[
                    whole(buffer.shape),
                    whole((2 * low_rank, model)),
                    pl.BlockSpec((2, low_rank, block), lambda f, *_: (0, 0, f)),
                    pl.BlockSpec((low_rank, block), lambda f, *_: (0, f)),
                    whole((low_rank, model)),
                ],
                scratch_shapes=[
                    wide,
                    pltpu.VMEM((slots, model), BF16),
                    pltpu.VMEM((slots, low_rank), BF16),
                    pltpu.VMEM((slots, model), F32),
                    pltpu.VMEM((slots, low_rank), F32),
                    pltpu.VMEM((slots, 2 * low_rank), F32),
                ],
            ),
            compiler_params=params(40),
            name="expert_backward",
        )(flags, *received, *others, *state, *weights)

    hops = [
        [(0, 1)],
        [(1, 2), (0, 1)],
        [(2, 3), (1, 2)],
        [(2, 3), (3, 2)],
        [(2, 1), (3, 2)],
        [(1, 0), (2, 1)],
        [(1, 0)],
    ]
    inputs, got, sent, mixed, adapter = {}, {}, {}, {}, {}
    state = None
    for tick in range(ticks):
        if tick == 0:
            sources = [tokens, cotangent]
        elif tick == 1:
            sources = [tokens, incoming, cotangent]
        else:
            sources = [incoming]
        kinds = {0: "FB", 1: "FB", 2: "F", 3: "F", 4: "FB"}.get(tick, "B")
        placed, inputs[tick] = dispatch(tick, kinds, sources)
        got[tick] = exchange(placed)
        if tick < forward_ticks:
            sent[tick], state = expert_forward(tick, got[tick], state)
            answer = sent[tick]
        if tick >= 3:
            received = [got[index] for index in {3: (0,), 4: (1, 4)}.get(tick, (tick,))]
            other = sent[{3: 3, 5: 3, 6: 4}[tick]] if tick in (3, 5, 6) else None
            answer, *adapter[tick] = expert_backward(tick, received, other, state)
        returned = exchange(answer)
        section_inputs = {4: (4, 2), 5: (3, 1), 6: (2, 0, 4), 7: (1,)}.get(tick, (tick,))
        grads = {3: [cotangent], 4: [cotangent, inputs[tick]]}.get(
            tick, [inputs[tick]] if tick > 4 else []
        )
        kinds = "F" if tick < 3 else "B" if tick in (4, 7) else "FB"
        mixed[tick] = combine(
            tick, kinds, returned, [inputs[index] for index in section_inputs], grads
        )
        if tick < ticks - 1:
            incoming = lax.ppermute(mixed[tick], "pipe", hops[tick])

    def by_rank(choices):
        value = choices[0]
        for rank in range(1, sections):
            value = jnp.where(section_index == rank, choices[rank], value)
        return value

    hidden = jnp.stack(
        [by_rank([mixed[m], mixed[1 + m], mixed[2 + m], mixed[5 + m]]) for m in range(micros)]
    )
    input_grads = jnp.stack([by_rank([mixed[6 - r + m] for r in range(4)]) for m in range(micros)])

    def summed(item):
        total = by_rank([adapter[6 - r][item] + adapter[7 - r][item] for r in range(4)]).astype(BF16)
        across = lax.ppermute(total, "dp", [(0, 1), (1, 0)])
        return total.astype(F32) + across.astype(F32)

    return (
        hidden[None],
        input_grads[None],
        summed(0).T[None, None],
        summed(1)[None, None],
        summed(2).T[None, None],
        summed(3)[None, None],
    )


def solution(mesh):
    placed = (
        P(None, ("expert", "dp"), None),
        P(None, ("expert", "dp"), None),
        P("pipe", None, ("expert", "dp"), None),
        P("pipe", None, ("expert", "dp"), None),
        P("pipe", None),
        P("pipe", "expert", None, None),
        P("pipe", "expert", None, None),
        P("pipe", "expert", None, None),
        P("pipe", "expert", None, None),
        P("pipe", "expert", None, None, None),
        P("pipe", "expert", None, None),
        P("pipe", "expert", None, None),
    )
    return jax.shard_map(
        body,
        mesh=mesh,
        in_specs=placed,
        out_specs=(
            P("pipe", None, ("expert", "dp"), None),
            P("pipe", None, ("expert", "dp"), None),
            P("pipe", "expert", None, None),
            P("pipe", "expert", None, None, None),
            P("pipe", "expert", None, None),
            P("pipe", "expert", None, None),
        ),
        check_vma=False,
    )
```

```python
import functools

import jax
import jax.numpy as jnp
import numpy as np
from jax import lax
from jax.experimental import pallas as pl
from jax.experimental.pallas import tpu as pltpu
from jax.sharding import PartitionSpec as P

EPS = 1e-06
SLOTS = 6
LANES = 128
F32 = jnp.float32
BF16 = jnp.bfloat16


def dot(left, right):
    return jnp.dot(left, right, preferred_element_type=F32)


def dot_nt(left, right):
    return lax.dot_general(left, right, (((1,), (1,)), ((), ())), preferred_element_type=F32)


def dot_tn(left, right):
    return lax.dot_general(left, right, (((0,), (0,)), ((), ())), preferred_element_type=F32)


def pack(read, out_ref, wide, peers, chunks):
    stride = SLOTS * chunks
    for slot in range(SLOTS):
        for chunk in range(chunks):
            wide[pl.ds(slot * chunks + chunk, peers, stride=stride), :] = read(slot, chunk)
    for peer in range(peers):
        out_ref[peer] = wide[peer * stride : (peer + 1) * stride, :].astype(BF16)


def pack_from(rows, out_ref, wide, peers, chunks):
    pack(
        lambda slot, chunk: rows[
            slot * peers : (slot + 1) * peers, chunk * LANES : (chunk + 1) * LANES
        ],
        out_ref,
        wide,
        peers,
        chunks,
    )


def unpack(in_ref, rows, wide, peers, chunks):
    stride = SLOTS * chunks
    for peer in range(peers):
        wide[peer * stride : (peer + 1) * stride, :] = in_ref[peer].astype(F32)
    for slot in range(SLOTS):
        for chunk in range(chunks):
            rows[slot * peers : (slot + 1) * peers, chunk * LANES : (chunk + 1) * LANES] = wide[
                pl.ds(slot * chunks + chunk, peers, stride=stride), :
            ].astype(BF16)


def split(weight):
    high = weight.astype(BF16)
    return high, (weight - high.astype(F32)).astype(BF16)


def tables_kernel(peers, routes, gates, place, scale_hi, scale_lo, pick, mix_hi, mix_lo):
    micros, _, rows = routes.shape
    slots = SLOTS * peers
    assert peers & (peers - 1) == 0
    number = lax.broadcasted_iota(jnp.int32, (slots, rows), 0)
    expert, position = number & (peers - 1), (number >> (peers.bit_length() - 1)).astype(F32)
    down = lax.broadcasted_iota(jnp.int32, (rows, rows), 0)
    across = lax.broadcasted_iota(jnp.int32, (rows, rows), 1)
    earlier = jnp.where(down < across, 1.0, 0.0).astype(BF16)
    for micro in range(micros):
        first = routes[micro, 0:1, :] == expert
        second = routes[micro, 1:2, :] == expert
        named = jnp.where(first | second, 1.0, 0.0)
        before = dot(named.astype(BF16), earlier)
        chosen = jnp.where(before == position, named, 0.0)
        weight = chosen * (
            jnp.where(first, gates[micro, 0:1, :], 0.0) + jnp.where(second, gates[micro, 1:2, :], 0.0)
        )
        place[micro] = chosen.astype(BF16)
        scale_hi[micro], scale_lo[micro] = split(weight)
        pick[micro] = chosen.T.astype(BF16)
        mix_hi[micro], mix_lo[micro] = split(weight.T)


def choose(refs, micro, which):
    blocks = [ref[...] if len(ref.shape) == 2 else ref[micro] for ref in refs]
    value = blocks[0]
    for index in range(1, len(blocks)):
        value = jnp.where(which == index, blocks[index], value)
    return value


def dispatch_kernel(dims, kinds, source_count, flags, *refs):
    peers, chunks, base, tick = dims
    sources = refs[:source_count]
    gain, place, scale_hi, scale_lo = refs[source_count : source_count + 4]
    out_ref = refs[source_count + 4]
    wide, rows = refs[-2:]
    is_forward, micro = flags[base], flags[base + 1]
    current = choose(sources, tick, flags[base + 2])
    if source_count > 1:
        refs[source_count + 5][...] = current

    def forward():
        values = current.astype(F32)
        inverse = lax.rsqrt(jnp.mean(values * values, axis=-1, keepdims=True) + EPS)
        rows[...] = dot(place[micro], (values * inverse * gain[...]).astype(BF16))

    def backward():
        rows[...] = dot(scale_hi[micro], current) + dot(scale_lo[micro], current)

    if kinds == "F":
        forward()
    elif kinds == "B":
        backward()
    else:
        pl.when(is_forward == 1)(forward)
        pl.when(is_forward == 0)(backward)
    pack_from(rows, out_ref, wide, peers, chunks)


def combine_kernel(dims, kinds, section_count, grad_count, flags, *refs):
    peers, chunks, base, grad_micro = dims
    returned = refs[0]
    sections = refs[1 : 1 + section_count]
    grads = refs[1 + section_count : 1 + section_count + grad_count]
    gain, pick, mix_hi, mix_lo, out_ref, wide, rows = refs[1 + section_count + grad_count :]
    is_forward, micro = flags[base], flags[base + 1]
    unpack(returned, rows, wide, peers, chunks)

    def forward():
        mixed = dot(mix_hi[micro], rows[...]) + dot(mix_lo[micro], rows[...])
        out_ref[...] = (choose(sections, 0, flags[base + 2]).astype(F32) + mixed).astype(BF16)

    def backward():
        section_in = choose(sections, 0, flags[base + 2]).astype(F32)
        grad_next = choose(grads, grad_micro, flags[base + 3]).astype(F32)
        inverse = lax.rsqrt(jnp.mean(section_in * section_in, axis=-1, keepdims=True) + EPS)
        scaled = dot(pick[micro], rows[...]) * gain[...]
        normed = section_in * inverse
        shared = jnp.mean(scaled * normed, axis=-1, keepdims=True)
        out_ref[...] = (grad_next + inverse * (scaled - normed * shared)).astype(BF16)

    if kinds == "F":
        forward()
    elif kinds == "B":
        backward()
    else:
        pl.when(is_forward == 1)(forward)
        pl.when(is_forward == 0)(backward)


def forward_kernel(
    dims, has_store, received, w_gate, w_up, w_down, in_a, in_b, down_a, down_b, *refs
):
    peers, chunks, low_rank, block, slot = dims
    sent, rows, low_in, gate_pre, up_pre, wide, total = refs[4 * has_store :]
    slots = rows.shape[1]
    unpack(received, rows.at[slot], wide, peers, chunks)
    slot_rows = rows[slot]
    low = dot_nt(slot_rows, in_a[...]).astype(BF16)
    low_in[slot] = low
    low_total = jnp.zeros((slots, low_rank), F32)
    for start in range(0, w_gate.shape[1], block):
        piece = pl.ds(start, block)
        gate = dot(slot_rows, w_gate[:, piece]) + dot(low[:, :low_rank], in_b[0, :, piece])
        up = dot(slot_rows, w_up[:, piece]) + dot(low[:, low_rank:], in_b[1, :, piece])
        gate_pre[slot, :, piece] = gate
        up_pre[slot, :, piece] = up
        activated = (gate * jax.nn.sigmoid(gate) * up).astype(BF16)
        low_total += dot_nt(activated, down_a[:, piece])
        part = dot(activated, w_down[piece, :])
        total[...] = part if start == 0 else total[...] + part
    total[...] += dot(low_total.astype(BF16), down_b[...])
    pack_from(total, sent, wide, peers, chunks)


def backward_kernel(dims, received_count, has_other, has_totals, flags, *refs):
    peers, chunks, low_rank, block, base = dims
    received = refs[:received_count]
    other = refs[received_count]
    refs = refs[received_count + has_other + 4 * has_totals :]
    (rows, low_in, gate_pre, up_pre, w_gate, w_up, w_down, in_a, in_b, down_a, down_b) = refs[:11]
    (sent, grad_in_a, grad_in_b, grad_down_a, grad_down_b) = refs[11:16]
    (wide, grad_out, total) = refs[16:]
    active, slot = flags[base] == 1, flags[base + 1]
    slots = rows.shape[1]

    def store(ref, where, value):
        ref[where] = jnp.where(flags[base + 3] == 1, ref[where] + value, value) if has_totals else value

    @pl.when(active)
    def _():
        if received_count == 1:
            unpack(received[0], grad_out, wide, peers, chunks)
        else:
            for index in range(received_count):

                @pl.when(flags[base + 2] == index)
                def _():
                    unpack(received[index], grad_out, wide, peers, chunks)

        grad = grad_out[...]
        grad_low_down = dot_nt(grad, down_b[...]).astype(BF16)
        low = low_in[slot]
        low_total = jnp.zeros((slots, low_rank), F32)
        gate_low = jnp.zeros((slots, low_rank), F32)
        up_low = jnp.zeros((slots, low_rank), F32)
        for start in range(0, w_gate.shape[1], block):
            piece = pl.ds(start, block)
            gate, up = gate_pre[slot, :, piece], up_pre[slot, :, piece]
            sigmoid = jax.nn.sigmoid(gate)
            silu = gate * sigmoid
            activated = (silu * up).astype(BF16)
            grad_act = dot_nt(grad, w_down[piece, :]) + dot(grad_low_down, down_a[:, piece])
            grad_gate = (grad_act * up * sigmoid * (1.0 + gate * (1.0 - sigmoid))).astype(BF16)
            grad_up = (grad_act * silu).astype(BF16)
            store(grad_in_b, (0, slice(None), piece), dot_tn(low[:, :low_rank], grad_gate))
            store(grad_in_b, (1, slice(None), piece), dot_tn(low[:, low_rank:], grad_up))
            store(grad_down_a, (slice(None), piece), dot_tn(grad_low_down, activated))
            low_total += dot_nt(activated, down_a[:, piece])
            gate_low += dot_nt(grad_gate, in_b[0, :, piece])
            up_low += dot_nt(grad_up, in_b[1, :, piece])
            part = dot_nt(grad_gate, w_gate[:, piece]) + dot_nt(grad_up, w_up[:, piece])
            total[...] = part if start == 0 else total[...] + part
        low_grad = jnp.concatenate([gate_low, up_low], axis=1).astype(BF16)
        total[...] += dot(low_grad, in_a[...])
        pack_from(total, sent, wide, peers, chunks)
        store(grad_in_a, ..., dot_tn(low_grad, rows[slot]))
        store(grad_down_b, ..., dot_tn(low_total.astype(BF16), grad))

    if has_other:

        @pl.when(jnp.logical_not(active))
        def _():
            sent[...] = other[...]


def params(megabytes):
    return pltpu.CompilerParams(vmem_limit_bytes=megabytes * 1024 * 1024)


def rank_flags(sections, micros):
    assert sections == 4 and micros == 2
    last = sections - 1
    ticks = 2 * sections
    table = np.zeros((sections, ticks, 12), np.int32)
    for rank in range(sections):
        for tick in range(ticks):
            row = table[rank, tick]
            forward = tick - rank if tick - rank in (0, 1) else None
            backward = tick - (2 * last - rank)
            backward = backward if backward in (0, 1) else None
            if forward is not None:
                row[0:2] = 1, forward
            elif backward is not None:
                row[0:2] = 0, backward
            elif rank == last and tick < 2:
                row[0:2] = 0, tick
            if tick == 0:
                row[2] = 1 if rank == last else 0
            elif tick == 1:
                row[2] = 2 if rank == last else (0 if rank == 0 else 1)
            if backward is not None:
                row[4:6] = 1, rank + backward
                row[6] = 0 if rank == last else 1
                row[7] = backward
                row[8:10] = 0, backward
            elif forward is not None:
                row[8:10] = 1, forward
            elif rank == last and tick in (5, 6):
                row[8:10] = 1, tick - 5
            if tick == 4:
                row[10:12] = (0, 0) if rank == last else (1, 1)
            elif tick == 5:
                row[10] = 1 if rank == 1 else 0
            elif tick == 6:
                row[10] = {1: 0, 0: 1, 3: 2}.get(rank, 0)
    return table.reshape(sections, -1)


def body(
    tokens, cotangent, routes, gates, norm_gain, w_gate, w_up, w_down, in_a, in_b, down_a, down_b
):
    section_index = lax.axis_index("pipe")
    sections = lax.axis_size("pipe")
    peers = lax.axis_size("expert")
    micros, tok_rows, model = tokens.shape
    hidden_width = w_gate.shape[3]
    low_rank = down_a.shape[3]
    slots = SLOTS * peers
    chunks = model // LANES
    ticks = 2 * sections
    forward_ticks = sections + micros - 1
    block = hidden_width // 3
    flags = lax.dynamic_index_in_dim(
        jnp.asarray(rank_flags(sections, micros)), section_index, 0, keepdims=False
    )
    w_gate, w_up, w_down = w_gate[0, 0], w_up[0, 0], w_down[0, 0]
    in_a, in_b, down_a, down_b = in_a[0, 0].T, in_b[0, 0], down_a[0, 0].T, down_b[0, 0]
    buffer = jax.ShapeDtypeStruct((peers, SLOTS * chunks, LANES), BF16)
    block_rows = jax.ShapeDtypeStruct((tok_rows, model), BF16)
    wide = pltpu.VMEM((peers * SLOTS * chunks, LANES), F32)

    routes, gates = routes[0], gates[0]
    held = pl.BlockSpec(memory_space=pltpu.VMEM)
    scalars = pl.BlockSpec(memory_space=pltpu.SMEM)
    table_in = jax.ShapeDtypeStruct((micros, slots, tok_rows), BF16)
    table_out = jax.ShapeDtypeStruct((micros, tok_rows, slots), BF16)
    place, scale_hi, scale_lo, pick, mix_hi, mix_lo = pl.pallas_call(
        functools.partial(tables_kernel, peers),
        out_shape=[table_in] * 3 + [table_out] * 3,
        in_specs=[held] * 2,
        out_specs=[held] * 6,
        compiler_params=params(8),
        name="tables",
    )(routes.transpose(0, 2, 1), gates.transpose(0, 2, 1))

    def exchange(rows):
        return lax.all_to_all(rows, "expert", split_axis=0, concat_axis=0, tiled=True)

    def dispatch(tick, kinds, sources):
        single = len(sources) == 1
        operands = [*sources, norm_gain, place, scale_hi, scale_lo]
        result = pl.pallas_call(
            functools.partial(
                dispatch_kernel, (peers, chunks, tick * 12, tick), kinds, len(sources)
            ),
            out_shape=[buffer] if single else [buffer, block_rows],
            in_specs=[scalars] + [held] * len(operands),
            out_specs=[held] * (1 if single else 2),
            scratch_shapes=[wide, pltpu.VMEM((slots, model), F32)],
            compiler_params=params(20),
            name="dispatch",
        )(flags, *operands)
        return result[0], sources[0] if single else result[1]

    def combine(tick, kinds, returned, section_inputs, grads):
        operands = [returned, *section_inputs, *grads, norm_gain, pick, mix_hi, mix_lo]
        return pl.pallas_call(
            functools.partial(
                combine_kernel,
                (peers, chunks, tick * 12 + 8, tick - sections + 1),
                kinds,
                len(section_inputs),
                len(grads),
            ),
            out_shape=block_rows,
            in_specs=[scalars] + [held] * len(operands),
            out_specs=held,
            scratch_shapes=[wide, pltpu.VMEM((slots, model), BF16)],
            compiler_params=params(20),
            name="combine",
        )(flags, *operands)

    weights = (w_gate, w_up, w_down, in_a, in_b, down_a, down_b)
    state_shapes = [
        jax.ShapeDtypeStruct((forward_ticks, slots, model), BF16),
        jax.ShapeDtypeStruct((forward_ticks, slots, 2 * low_rank), BF16),
        jax.ShapeDtypeStruct((forward_ticks, slots, hidden_width), F32),
        jax.ShapeDtypeStruct((forward_ticks, slots, hidden_width), F32),
    ]

    def expert_forward(tick, received, state):
        has_store = state is not None
        result = pl.pallas_call(
            functools.partial(forward_kernel, (peers, chunks, low_rank, block, tick), has_store),
            out_shape=[buffer] + state_shapes,
            in_specs=[held] * (12 if has_store else 8),
            out_specs=[held] * 5,
            scratch_shapes=[wide, pltpu.VMEM((slots, model), F32)],
            input_output_aliases={8: 1, 9: 2, 10: 3, 11: 4} if has_store else {},
            compiler_params=params(20),
            name="expert_forward",
        )(received, *weights, *(state if has_store else ()))
        return result[0], result[1:]

    def expert_backward(tick, received, other, state, totals):
        base = tick * 12 + 4
        others = [] if other is None else [other]
        operands = [*received, *others, *totals, *state, *weights]
        first = 1 + len(received) + len(others)
        return pl.pallas_call(
            functools.partial(
                backward_kernel,
                (peers, chunks, low_rank, block, base),
                len(received),
                len(others),
                len(totals) > 0,
            ),
            out_shape=[
                buffer,
                jax.ShapeDtypeStruct((2 * low_rank, model), F32),
                jax.ShapeDtypeStruct((2, low_rank, hidden_width), F32),
                jax.ShapeDtypeStruct((low_rank, hidden_width), F32),
                jax.ShapeDtypeStruct((low_rank, model), F32),
            ],
            in_specs=[scalars] + [held] * len(operands),
            out_specs=[held] * 5,
            input_output_aliases={first + item: 1 + item for item in range(len(totals))},
            scratch_shapes=[
                wide,
                pltpu.VMEM((slots, model), BF16),
                pltpu.VMEM((slots, model), F32),
            ],
            compiler_params=params(20),
            name="expert_backward",
        )(flags, *operands)

    hops = [
        [(0, 1)],
        [(1, 2), (0, 1)],
        [(2, 3), (1, 2)],
        [(2, 3), (3, 2)],
        [(2, 1), (3, 2)],
        [(1, 0), (2, 1)],
        [(1, 0)],
    ]
    inputs, got, sent, mixed = {}, {}, {}, {}
    state, totals = None, ()
    for tick in range(ticks):
        if tick == 0:
            sources = [tokens, cotangent]
        elif tick == 1:
            sources = [tokens, incoming, cotangent]
        else:
            sources = [incoming]
        kinds = {0: "FB", 1: "FB", 2: "F", 3: "F", 4: "FB"}.get(tick, "B")
        placed, inputs[tick] = dispatch(tick, kinds, sources)
        got[tick] = exchange(placed)
        if tick < forward_ticks:
            sent[tick], state = expert_forward(tick, got[tick], state)
            answer = sent[tick]
        if tick >= 3:
            received = [got[index] for index in {3: (0,), 4: (1, 4)}.get(tick, (tick,))]
            other = sent[{3: 3, 5: 3, 6: 4}[tick]] if tick in (3, 5, 6) else None
            answer, *totals = expert_backward(tick, received, other, state, totals)
        returned = exchange(answer)
        section_inputs = {4: (4, 2), 5: (3, 1), 6: (2, 0, 4), 7: (1,)}.get(tick, (tick,))
        grads = {3: [cotangent], 4: [cotangent, inputs[tick]]}.get(
            tick, [inputs[tick]] if tick > 4 else []
        )
        kinds = "F" if tick < 3 else "B" if tick in (4, 7) else "FB"
        mixed[tick] = combine(
            tick, kinds, returned, [inputs[index] for index in section_inputs], grads
        )
        if tick < ticks - 1:
            incoming = lax.ppermute(mixed[tick], "pipe", hops[tick])

    mixed, totals = lax.optimization_barrier((mixed, totals))

    def by_rank(choices):
        value = choices[0]
        for rank in range(1, sections):
            value = jnp.where(section_index == rank, choices[rank], value)
        return value

    def summed(total):
        total = total.astype(BF16)
        across = lax.ppermute(total, "dp", [(0, 1), (1, 0)])
        return total.astype(F32) + across.astype(F32)

    totals = [summed(total) for total in totals]
    hidden = jnp.stack(
        [by_rank([mixed[m], mixed[1 + m], mixed[2 + m], mixed[5 + m]]) for m in range(micros)]
    )
    input_grads = jnp.stack([by_rank([mixed[6 - r + m] for r in range(4)]) for m in range(micros)])
    return (
        hidden[None],
        input_grads[None],
        totals[0].T[None, None],
        totals[1][None, None],
        totals[2].T[None, None],
        totals[3][None, None],
    )


def solution(mesh):
    placed = (
        P(None, ("expert", "dp"), None),
        P(None, ("expert", "dp"), None),
        P("pipe", None, ("expert", "dp"), None),
        P("pipe", None, ("expert", "dp"), None),
        P("pipe", None),
        P("pipe", "expert", None, None),
        P("pipe", "expert", None, None),
        P("pipe", "expert", None, None),
        P("pipe", "expert", None, None),
        P("pipe", "expert", None, None, None),
        P("pipe", "expert", None, None),
        P("pipe", "expert", None, None),
    )
    return jax.shard_map(
        body,
        mesh=mesh,
        in_specs=placed,
        out_specs=(
            P("pipe", None, ("expert", "dp"), None),
            P("pipe", None, ("expert", "dp"), None),
            P("pipe", "expert", None, None),
            P("pipe", "expert", None, None, None),
            P("pipe", "expert", None, None),
            P("pipe", "expert", None, None),
        ),
        check_vma=False,
    )
```

```python
import functools

import jax
import jax.numpy as jnp
import numpy as np
from jax import lax
from jax.experimental import pallas as pl
from jax.experimental.pallas import tpu as pltpu
from jax.sharding import PartitionSpec as P

EPS = 1e-06
SLOTS = 6
LANES = 128
F32 = jnp.float32
BF16 = jnp.bfloat16


def dot(left, right):
    return jnp.dot(left, right, preferred_element_type=F32)


def dot_nt(left, right):
    return lax.dot_general(left, right, (((1,), (1,)), ((), ())), preferred_element_type=F32)


def dot_tn(left, right):
    return lax.dot_general(left, right, (((0,), (0,)), ((), ())), preferred_element_type=F32)


def pack(columns, out_ref, wide, peers, chunks):
    stride = SLOTS * chunks
    step = 4
    for first in range(0, chunks, step):
        block = columns(first * LANES, step * LANES)
        for slot in range(SLOTS):
            for chunk in range(step):
                wide[pl.ds(slot * chunks + first + chunk, peers, stride=stride), :] = block[
                    slot * peers : (slot + 1) * peers, chunk * LANES : (chunk + 1) * LANES
                ]
    for peer in range(peers):
        out_ref[peer] = wide[peer * stride : (peer + 1) * stride, :].astype(BF16)


def unpack(in_ref, rows, wide, peers, chunks):
    stride = SLOTS * chunks
    for peer in range(peers):
        wide[peer * stride : (peer + 1) * stride, :] = in_ref[peer].astype(F32)
    for slot in range(SLOTS):
        for chunk in range(chunks):
            rows[slot * peers : (slot + 1) * peers, chunk * LANES : (chunk + 1) * LANES] = wide[
                pl.ds(slot * chunks + chunk, peers, stride=stride), :
            ].astype(BF16)


def split(weight):
    high = weight.astype(BF16)
    return high, (weight - high.astype(F32)).astype(BF16)


def make_tables(peers, routes, gates, place, scale_hi, scale_lo, pick, mix_hi, mix_lo):
    micros, _, rows = routes.shape
    slots = SLOTS * peers
    assert peers & (peers - 1) == 0
    number = lax.broadcasted_iota(jnp.int32, (slots, rows), 0)
    expert, position = number & (peers - 1), (number >> (peers.bit_length() - 1)).astype(F32)
    down = lax.broadcasted_iota(jnp.int32, (rows, rows), 0)
    across = lax.broadcasted_iota(jnp.int32, (rows, rows), 1)
    earlier = jnp.where(down < across, 1.0, 0.0).astype(BF16)
    for micro in range(micros):
        first = routes[micro, 0:1, :] == expert
        second = routes[micro, 1:2, :] == expert
        named = jnp.where(first | second, 1.0, 0.0)
        before = dot(named.astype(BF16), earlier)
        chosen = jnp.where(before == position, named, 0.0)
        weight = chosen * (
            jnp.where(first, gates[micro, 0:1, :], 0.0) + jnp.where(second, gates[micro, 1:2, :], 0.0)
        )
        place[micro] = chosen.astype(BF16)
        scale_hi[micro], scale_lo[micro] = split(weight)
        pick[micro] = chosen.T.astype(BF16)
        mix_hi[micro], mix_lo[micro] = split(weight.T)


def choose(refs, micro, which):
    blocks = [ref[...] if len(ref.shape) == 2 else ref[micro] for ref in refs]
    value = blocks[0]
    for index in range(1, len(blocks)):
        value = jnp.where(which == index, blocks[index], value)
    return value


def dispatch_rows(dims, kinds, current, flags, gain, place, scale_hi, scale_lo, out_ref, wide, rows):
    peers, chunks, base = dims
    is_forward, micro = flags[base], flags[base + 1]

    def forward():
        values = current.astype(F32)
        inverse = lax.rsqrt(jnp.mean(values * values, axis=-1, keepdims=True) + EPS)
        rows[...] = (values * inverse * gain[...]).astype(BF16)
        pack(
            lambda start, size: dot(place[micro], rows[:, start : start + size]),
            out_ref,
            wide,
            peers,
            chunks,
        )

    def backward():
        rows[...] = current
        pack(
            lambda start, size: dot(scale_hi[micro], rows[:, start : start + size])
            + dot(scale_lo[micro], rows[:, start : start + size]),
            out_ref,
            wide,
            peers,
            chunks,
        )

    if kinds == "F":
        forward()
    elif kinds == "B":
        backward()
    else:
        pl.when(is_forward == 1)(forward)
        pl.when(is_forward == 0)(backward)


def dispatch_kernel(dims, kinds, source_count, flags, *refs):
    peers, chunks, base, tick = dims
    sources = refs[:source_count]
    gain, place, scale_hi, scale_lo, out_ref = refs[source_count : source_count + 5]
    wide, rows = refs[-2:]
    current = choose(sources, tick, flags[base + 2])
    if source_count > 1:
        refs[source_count + 5][...] = current
    dispatch_rows(
        (peers, chunks, base),
        kinds,
        current,
        flags,
        gain,
        place,
        scale_hi,
        scale_lo,
        out_ref,
        wide,
        rows,
    )


def opening_kernel(dims, flags, routes, gates, tokens, cotangent, gain, *refs):
    peers, chunks = dims
    tables, out_ref, first, wide, rows = refs[:6], *refs[6:]
    make_tables(peers, routes, gates, *tables)
    current = choose([tokens, cotangent], 0, flags[2])
    first[...] = current
    dispatch_rows(
        (peers, chunks, 0), "FB", current, flags, gain, *tables[:3], out_ref, wide, rows
    )


def combine_kernel(dims, kinds, section_count, grad_count, has_final, flags, *refs):
    peers, chunks, base, grad_micro = dims
    returned = refs[0]
    sections = refs[1 : 1 + section_count]
    grads = refs[1 + section_count : 1 + section_count + grad_count]
    gain, pick, mix_hi, mix_lo = refs[1 + section_count + grad_count :][:4]
    out_ref, wide, rows = refs[-3:]
    is_forward, micro = flags[base], flags[base + 1]
    unpack(returned, rows, wide, peers, chunks)

    def forward():
        mixed = dot(mix_hi[micro], rows[...]) + dot(mix_lo[micro], rows[...])
        out_ref[...] = (choose(sections, 0, flags[base + 2]).astype(F32) + mixed).astype(BF16)

    def backward():
        section_in = choose(sections, 0, flags[base + 2]).astype(F32)
        grad_next = choose(grads, grad_micro, flags[base + 3]).astype(F32)
        inverse = lax.rsqrt(jnp.mean(section_in * section_in, axis=-1, keepdims=True) + EPS)
        scaled = dot(pick[micro], rows[...]) * gain[...]
        normed = section_in * inverse
        shared = jnp.mean(scaled * normed, axis=-1, keepdims=True)
        result = (grad_next + inverse * (scaled - normed * shared)).astype(BF16)
        if has_final:
            final = refs[-4]
            out_ref[...] = final[...]

            @pl.when(flags[base + 2 - 6] == 1)
            def _():
                out_ref[1] = result

        else:
            out_ref[...] = result

    if kinds == "F":
        forward()
    elif kinds == "B":
        backward()
    else:
        pl.when(is_forward == 1)(forward)
        pl.when(is_forward == 0)(backward)


def assemble_kernel(flags, *refs):
    mixed, (hidden, input_grads) = refs[:-2], refs[-2:]
    for micro in range(hidden.shape[0]):
        kept = [mixed[micro], mixed[1 + micro], mixed[2 + micro], mixed[5 + micro]]
        hidden[micro] = choose(kept, 0, flags[3])
        kept = [mixed[min(6, 6 + micro - rank)] for rank in range(4)]
        input_grads[micro] = choose(kept, 0, flags[3])


def sum_kernel(*refs):
    count = len(refs) // 3
    for own, other, out in zip(refs[:count], refs[count : 2 * count], refs[2 * count :]):
        out[...] = own[...].astype(F32) + other[...].astype(F32)


def forward_kernel(
    dims, has_store, received, w_gate, w_up, w_down, in_a, in_b, down_a, down_b, *refs
):
    peers, chunks, low_rank, block, slot = dims
    sent, rows, low_in, gate_pre, up_pre, wide, acts = refs[4 * has_store :]
    slots = rows.shape[1]
    unpack(received, rows.at[slot], wide, peers, chunks)
    slot_rows = rows[slot]
    low = dot_nt(slot_rows, in_a[...]).astype(BF16)
    low_in[slot] = low
    low_total = jnp.zeros((slots, low_rank), F32)
    for start in range(0, w_gate.shape[1], block):
        piece = pl.ds(start, block)
        gate = dot(slot_rows, w_gate[:, piece]) + dot(low[:, :low_rank], in_b[0, :, piece])
        up = dot(slot_rows, w_up[:, piece]) + dot(low[:, low_rank:], in_b[1, :, piece])
        gate_pre[slot, :, piece] = gate
        up_pre[slot, :, piece] = up
        activated = (gate * jax.nn.sigmoid(gate) * up).astype(BF16)
        low_total += dot_nt(activated, down_a[:, piece])
        acts[:, piece] = activated
    low_down = low_total.astype(BF16)
    pack(
        lambda start, size: dot(acts[...], w_down[:, start : start + size])
        + dot(low_down, down_b[:, start : start + size]),
        sent,
        wide,
        peers,
        chunks,
    )


def backward_kernel(dims, received_count, has_other, has_totals, is_last, flags, *refs):
    peers, chunks, low_rank, block, base = dims
    received = refs[:received_count]
    other = refs[received_count]
    refs = refs[received_count + has_other + 4 * has_totals :]
    (rows, low_in, gate_pre, up_pre, w_gate, w_up, w_down, in_a, in_b, down_a, down_b) = refs[:11]
    (sent, grad_in_a, grad_in_b, grad_down_a, grad_down_b) = refs[11:16]
    (wide, grad_out, total) = refs[-3:]
    active, slot = flags[base] == 1, flags[base + 1]
    slots = rows.shape[1]

    def store(ref, where, value):
        ref[where] = jnp.where(flags[base + 3] == 1, ref[where] + value, value) if has_totals else value

    @pl.when(active)
    def _():
        if received_count == 1:
            unpack(received[0], grad_out, wide, peers, chunks)
        else:
            for index in range(received_count):

                @pl.when(flags[base + 2] == index)
                def _():
                    unpack(received[index], grad_out, wide, peers, chunks)

        grad = grad_out[...]
        grad_low_down = dot_nt(grad, down_b[...]).astype(BF16)
        low = low_in[slot]
        low_total = jnp.zeros((slots, low_rank), F32)
        gate_low = jnp.zeros((slots, low_rank), F32)
        up_low = jnp.zeros((slots, low_rank), F32)
        for start in range(0, w_gate.shape[1], block):
            piece = pl.ds(start, block)
            gate, up = gate_pre[slot, :, piece], up_pre[slot, :, piece]
            sigmoid = jax.nn.sigmoid(gate)
            silu = gate * sigmoid
            activated = (silu * up).astype(BF16)
            grad_act = dot_nt(grad, w_down[piece, :]) + dot(grad_low_down, down_a[:, piece])
            grad_gate = (grad_act * up * sigmoid * (1.0 + gate * (1.0 - sigmoid))).astype(BF16)
            grad_up = (grad_act * silu).astype(BF16)
            store(grad_in_b, (0, slice(None), piece), dot_tn(low[:, :low_rank], grad_gate))
            store(grad_in_b, (1, slice(None), piece), dot_tn(low[:, low_rank:], grad_up))
            store(grad_down_a, (slice(None), piece), dot_tn(grad_low_down, activated))
            low_total += dot_nt(activated, down_a[:, piece])
            gate_low += dot_nt(grad_gate, in_b[0, :, piece])
            up_low += dot_nt(grad_up, in_b[1, :, piece])
            part = dot_nt(grad_gate, w_gate[:, piece]) + dot_nt(grad_up, w_up[:, piece])
            total[...] = part if start == 0 else total[...] + part
        low_grad = jnp.concatenate([gate_low, up_low], axis=1).astype(BF16)
        pack(
            lambda start, size: total[:, start : start + size]
            + dot(low_grad, in_a[:, start : start + size]),
            sent,
            wide,
            peers,
            chunks,
        )
        store(grad_in_a, ..., dot_tn(low_grad, rows[slot]))
        store(grad_down_b, ..., dot_tn(low_total.astype(BF16), grad))

    if has_other:

        @pl.when(jnp.logical_not(active))
        def _():
            sent[...] = other[...]

    if is_last:
        for total, rounded in zip(refs[12:16], refs[16:20]):
            rounded[...] = total[...].astype(BF16)


def params(megabytes):
    return pltpu.CompilerParams(vmem_limit_bytes=megabytes * 1024 * 1024)


def rank_flags(sections, micros):
    assert sections == 4 and micros == 2
    last = sections - 1
    ticks = 2 * sections
    table = np.zeros((sections, ticks, 12), np.int32)
    for rank in range(sections):
        for tick in range(ticks):
            row = table[rank, tick]
            row[3] = rank
            forward = tick - rank if tick - rank in (0, 1) else None
            backward = tick - (2 * last - rank)
            backward = backward if backward in (0, 1) else None
            if forward is not None:
                row[0:2] = 1, forward
            elif backward is not None:
                row[0:2] = 0, backward
            elif rank == last and tick < 2:
                row[0:2] = 0, tick
            if tick == 0:
                row[2] = 1 if rank == last else 0
            elif tick == 1:
                row[2] = 2 if rank == last else (0 if rank == 0 else 1)
            if backward is not None:
                row[4:6] = 1, rank + backward
                row[6] = 0 if rank == last else 1
                row[7] = backward
                row[8:10] = 0, backward
            elif forward is not None:
                row[8:10] = 1, forward
            elif rank == last and tick in (5, 6):
                row[8:10] = 1, tick - 5
            if tick == 4:
                row[10:12] = (0, 0) if rank == last else (1, 1)
            elif tick == 5:
                row[10] = 1 if rank == 1 else 0
            elif tick == 6:
                row[10] = {1: 0, 0: 1, 3: 2}.get(rank, 0)
    return table.reshape(sections, -1)


def body(
    tokens, cotangent, routes, gates, norm_gain, w_gate, w_up, w_down, in_a, in_b, down_a, down_b
):
    section_index = lax.axis_index("pipe")
    sections = lax.axis_size("pipe")
    peers = lax.axis_size("expert")
    micros, tok_rows, model = tokens.shape
    hidden_width = w_gate.shape[3]
    low_rank = down_a.shape[3]
    slots = SLOTS * peers
    chunks = model // LANES
    ticks = 2 * sections
    forward_ticks = sections + micros - 1
    block = hidden_width // 3
    flags = lax.dynamic_index_in_dim(
        jnp.asarray(rank_flags(sections, micros)), section_index, 0, keepdims=False
    )
    w_gate, w_up, w_down = w_gate[0, 0], w_up[0, 0], w_down[0, 0]
    in_a, in_b, down_a, down_b = in_a[0, 0].T, in_b[0, 0], down_a[0, 0].T, down_b[0, 0]
    buffer = jax.ShapeDtypeStruct((peers, SLOTS * chunks, LANES), BF16)
    block_rows = jax.ShapeDtypeStruct((tok_rows, model), BF16)
    wide = pltpu.VMEM((peers * SLOTS * chunks, LANES), F32)

    routes, gates = routes[0], gates[0]
    held = pl.BlockSpec(memory_space=pltpu.VMEM)
    scalars = pl.BlockSpec(memory_space=pltpu.SMEM)
    table_in = jax.ShapeDtypeStruct((micros, slots, tok_rows), BF16)
    table_out = jax.ShapeDtypeStruct((micros, tok_rows, slots), BF16)
    *tables, placed_first, input_first = pl.pallas_call(
        functools.partial(opening_kernel, (peers, chunks)),
        out_shape=[table_in] * 3 + [table_out] * 3 + [buffer, block_rows],
        in_specs=[scalars] + [held] * 5,
        out_specs=[held] * 8,
        scratch_shapes=[wide, pltpu.VMEM((tok_rows, model), BF16)],
        compiler_params=params(20),
        name="opening",
    )(flags, routes.transpose(0, 2, 1), gates.transpose(0, 2, 1), tokens, cotangent, norm_gain)
    place, scale_hi, scale_lo, pick, mix_hi, mix_lo = tables
    weights = (w_gate, w_up, w_down, in_a, in_b, down_a, down_b)

    def exchange(rows):
        return lax.all_to_all(rows, "expert", split_axis=0, concat_axis=0, tiled=True)

    def dispatch(tick, kinds, sources):
        single = len(sources) == 1
        operands = [*sources, norm_gain, place, scale_hi, scale_lo]
        result = pl.pallas_call(
            functools.partial(
                dispatch_kernel, (peers, chunks, tick * 12, tick), kinds, len(sources)
            ),
            out_shape=[buffer] if single else [buffer, block_rows],
            in_specs=[scalars] + [held] * len(operands),
            out_specs=[held] * (1 if single else 2),
            scratch_shapes=[wide, pltpu.VMEM((tok_rows, model), BF16)],
            compiler_params=params(20),
            name="dispatch",
        )(flags, *operands)
        return result[0], sources[0] if single else result[1]

    def combine(tick, kinds, returned, section_inputs, grads, final):
        finals = [] if final is None else [final]
        operands = [returned, *section_inputs, *grads, norm_gain, pick, mix_hi, mix_lo, *finals]
        return pl.pallas_call(
            functools.partial(
                combine_kernel,
                (peers, chunks, tick * 12 + 8, tick - sections + 1),
                kinds,
                len(section_inputs),
                len(grads),
                len(finals) > 0,
            ),
            out_shape=block_rows if final is None else jax.ShapeDtypeStruct(final.shape, BF16),
            in_specs=[scalars] + [held] * len(operands),
            out_specs=held,
            input_output_aliases={len(operands): 0} if finals else {},
            scratch_shapes=[wide, pltpu.VMEM((slots, model), BF16)],
            compiler_params=params(20),
            name="combine",
        )(flags, *operands)

    state_shapes = [
        jax.ShapeDtypeStruct((forward_ticks, slots, model), BF16),
        jax.ShapeDtypeStruct((forward_ticks, slots, 2 * low_rank), BF16),
        jax.ShapeDtypeStruct((forward_ticks, slots, hidden_width), F32),
        jax.ShapeDtypeStruct((forward_ticks, slots, hidden_width), F32),
    ]

    def expert_forward(tick, received, state):
        has_store = state is not None
        result = pl.pallas_call(
            functools.partial(forward_kernel, (peers, chunks, low_rank, block, tick), has_store),
            out_shape=[buffer] + state_shapes,
            in_specs=[held] * (12 if has_store else 8),
            out_specs=[held] * 5,
            scratch_shapes=[wide, pltpu.VMEM((slots, hidden_width), BF16)],
            input_output_aliases={8: 1, 9: 2, 10: 3, 11: 4} if has_store else {},
            compiler_params=params(20),
            name="expert_forward",
        )(received, *weights, *(state if has_store else ()))
        return result[0], result[1:]

    def expert_backward(tick, received, other, state, totals):
        base = tick * 12 + 4
        others = [] if other is None else [other]
        operands = [*received, *others, *totals, *state, *weights]
        first = 1 + len(received) + len(others)
        is_last = tick == ticks - 1
        sums = [
            (2 * low_rank, model),
            (2, low_rank, hidden_width),
            (low_rank, hidden_width),
            (low_rank, model),
        ]
        return pl.pallas_call(
            functools.partial(
                backward_kernel,
                (peers, chunks, low_rank, block, base),
                len(received),
                len(others),
                len(totals) > 0,
                is_last,
            ),
            out_shape=[buffer]
            + [jax.ShapeDtypeStruct(shape, F32) for shape in sums]
            + [jax.ShapeDtypeStruct(shape, BF16) for shape in sums * is_last],
            in_specs=[scalars] + [held] * len(operands),
            out_specs=[held] * (9 if is_last else 5),
            input_output_aliases={first + item: 1 + item for item in range(len(totals))},
            scratch_shapes=[
                wide,
                pltpu.VMEM((slots, model), BF16),
                pltpu.VMEM((slots, model), F32),
            ],
            compiler_params=params(20),
            name="expert_backward",
        )(flags, *operands)

    hops = [
        [(0, 1)],
        [(1, 2), (0, 1)],
        [(2, 3), (1, 2)],
        [(2, 3), (3, 2)],
        [(2, 1), (3, 2)],
        [(1, 0), (2, 1)],
        [(1, 0)],
    ]
    inputs, got, sent, mixed = {}, {}, {}, {}
    state, totals = None, ()
    for tick in range(ticks):
        if tick == 1:
            sources = [tokens, incoming, cotangent]
        elif tick > 1:
            sources = [incoming]
        kinds = {1: "FB", 2: "F", 3: "F", 4: "FB"}.get(tick, "B")
        if tick == 0:
            placed, inputs[tick] = placed_first, input_first
        else:
            placed, inputs[tick] = dispatch(tick, kinds, sources)
        got[tick] = exchange(placed)
        if tick < forward_ticks:
            sent[tick], state = expert_forward(tick, got[tick], state)
            answer = sent[tick]
        if tick >= 3:
            received = [got[index] for index in {3: (0,), 4: (1, 4)}.get(tick, (tick,))]
            other = sent[{3: 3, 5: 3, 6: 4}[tick]] if tick in (3, 5, 6) else None
            answer, *totals = expert_backward(tick, received, other, state, totals)
        returned = exchange(answer)
        if tick == ticks - 1:
            returned, rounded = lax.optimization_barrier((returned, totals[4:]))
        section_inputs = {4: (4, 2), 5: (3, 1), 6: (2, 0, 4), 7: (1,)}.get(tick, (tick,))
        grads = {3: [cotangent], 4: [cotangent, inputs[tick]]}.get(
            tick, [inputs[tick]] if tick > 4 else []
        )
        kinds = "F" if tick < 3 else "B" if tick in (4, 7) else "FB"
        final = input_grads if tick == ticks - 1 else None
        mixed[tick] = combine(
            tick, kinds, returned, [inputs[index] for index in section_inputs], grads, final
        )
        if tick < ticks - 1:
            incoming = lax.ppermute(mixed[tick], "pipe", hops[tick])
        if tick == ticks - 2:
            pair = jax.ShapeDtypeStruct((micros, tok_rows, model), BF16)
            hidden, input_grads = pl.pallas_call(
                assemble_kernel,
                out_shape=[pair] * 2,
                in_specs=[scalars] + [held] * (ticks - 1),
                out_specs=[held] * 2,
                compiler_params=params(8),
                name="assemble",
            )(flags, *[mixed[index] for index in range(ticks - 1)])
            incoming, hidden, input_grads = lax.optimization_barrier(
                (incoming, hidden, input_grads)
            )

    input_grads = mixed[ticks - 1]

    across = [lax.ppermute(total, "dp", [(0, 1), (1, 0)]) for total in rounded]
    totals = pl.pallas_call(
        sum_kernel,
        out_shape=[jax.ShapeDtypeStruct(total.shape, F32) for total in rounded],
        in_specs=[held] * (2 * len(rounded)),
        out_specs=[held] * len(rounded),
        compiler_params=params(8),
        name="sums",
    )(*rounded, *across)
    return (
        hidden[None],
        input_grads[None],
        totals[0].T[None, None],
        totals[1][None, None],
        totals[2].T[None, None],
        totals[3][None, None],
    )


def solution(mesh):
    placed = (
        P(None, ("expert", "dp"), None),
        P(None, ("expert", "dp"), None),
        P("pipe", None, ("expert", "dp"), None),
        P("pipe", None, ("expert", "dp"), None),
        P("pipe", None),
        P("pipe", "expert", None, None),
        P("pipe", "expert", None, None),
        P("pipe", "expert", None, None),
        P("pipe", "expert", None, None),
        P("pipe", "expert", None, None, None),
        P("pipe", "expert", None, None),
        P("pipe", "expert", None, None),
    )
    return jax.shard_map(
        body,
        mesh=mesh,
        in_specs=placed,
        out_specs=(
            P("pipe", None, ("expert", "dp"), None),
            P("pipe", None, ("expert", "dp"), None),
            P("pipe", "expert", None, None),
            P("pipe", "expert", None, None, None),
            P("pipe", "expert", None, None),
            P("pipe", "expert", None, None),
        ),
        check_vma=False,
    )
```

```python
import functools

import jax
import jax.numpy as jnp
import numpy as np
from jax import lax
from jax.experimental import pallas as pl
from jax.experimental.pallas import tpu as pltpu
from jax.sharding import PartitionSpec as P

EPS = 1e-06
SLOTS = 6
LANES = 128
F32 = jnp.float32
BF16 = jnp.bfloat16


def dot(left, right):
    return jnp.dot(left, right, preferred_element_type=F32)


def dot_nt(left, right):
    return lax.dot_general(left, right, (((1,), (1,)), ((), ())), preferred_element_type=F32)


def dot_tn(left, right):
    return lax.dot_general(left, right, (((0,), (0,)), ((), ())), preferred_element_type=F32)


def pack(columns, out_ref, wide, peers, chunks):
    stride = SLOTS * chunks
    step = 4
    for first in range(0, chunks, step):
        block = columns(first * LANES, step * LANES)
        for slot in range(SLOTS):
            for chunk in range(step):
                wide[pl.ds(slot * chunks + first + chunk, peers, stride=stride), :] = block[
                    slot * peers : (slot + 1) * peers, chunk * LANES : (chunk + 1) * LANES
                ]
    for peer in range(peers):
        out_ref[peer] = wide[peer * stride : (peer + 1) * stride, :].astype(BF16)


def unpack(in_ref, rows, wide, peers, chunks):
    stride = SLOTS * chunks
    for peer in range(peers):
        wide[peer * stride : (peer + 1) * stride, :] = in_ref[peer].astype(F32)
    for slot in range(SLOTS):
        for chunk in range(chunks):
            rows[slot * peers : (slot + 1) * peers, chunk * LANES : (chunk + 1) * LANES] = wide[
                pl.ds(slot * chunks + chunk, peers, stride=stride), :
            ].astype(BF16)


def split(weight):
    high = weight.astype(BF16)
    return high, (weight - high.astype(F32)).astype(BF16)


def make_tables(peers, routes, gates, place, scale_hi, scale_lo, pick, mix_hi, mix_lo):
    micros, _, rows = routes.shape
    slots = SLOTS * peers
    assert peers & (peers - 1) == 0
    number = lax.broadcasted_iota(jnp.int32, (slots, rows), 0)
    expert, position = number & (peers - 1), (number >> (peers.bit_length() - 1)).astype(F32)
    down = lax.broadcasted_iota(jnp.int32, (rows, rows), 0)
    across = lax.broadcasted_iota(jnp.int32, (rows, rows), 1)
    earlier = jnp.where(down < across, 1.0, 0.0).astype(BF16)
    for micro in range(micros):
        first = routes[micro, 0:1, :] == expert
        second = routes[micro, 1:2, :] == expert
        named = jnp.where(first | second, 1.0, 0.0)
        before = dot(named.astype(BF16), earlier)
        chosen = jnp.where(before == position, named, 0.0)
        weight = chosen * (
            jnp.where(first, gates[micro, 0:1, :], 0.0) + jnp.where(second, gates[micro, 1:2, :], 0.0)
        )
        place[micro] = chosen.astype(BF16)
        scale_hi[micro], scale_lo[micro] = split(weight)
        pick[micro] = chosen.T.astype(BF16)
        mix_hi[micro], mix_lo[micro] = split(weight.T)


def choose(refs, micro, which):
    blocks = [ref[...] if len(ref.shape) == 2 else ref[micro] for ref in refs]
    value = blocks[0]
    for index in range(1, len(blocks)):
        value = jnp.where(which == index, blocks[index], value)
    return value


def dispatch_rows(dims, kinds, current, flags, gain, place, scale_hi, scale_lo, out_ref, wide, rows):
    peers, chunks, base = dims
    is_forward, micro = flags[base], flags[base + 1]

    def forward():
        values = current.astype(F32)
        inverse = lax.rsqrt(jnp.mean(values * values, axis=-1, keepdims=True) + EPS)
        rows[...] = (values * inverse * gain[...]).astype(BF16)
        pack(
            lambda start, size: dot(place[micro], rows[:, start : start + size]),
            out_ref,
            wide,
            peers,
            chunks,
        )

    def backward():
        rows[...] = current
        pack(
            lambda start, size: dot(scale_hi[micro], rows[:, start : start + size])
            + dot(scale_lo[micro], rows[:, start : start + size]),
            out_ref,
            wide,
            peers,
            chunks,
        )

    if kinds == "F":
        forward()
    elif kinds == "B":
        backward()
    else:
        pl.when(is_forward == 1)(forward)
        pl.when(is_forward == 0)(backward)


def dispatch_kernel(dims, kinds, source_count, flags, *refs):
    peers, chunks, base, tick = dims
    sources = refs[:source_count]
    gain, place, scale_hi, scale_lo, out_ref = refs[source_count : source_count + 5]
    wide, rows = refs[-2:]
    current = choose(sources, tick, flags[base + 2])
    if source_count > 1:
        refs[source_count + 5][...] = current
    dispatch_rows(
        (peers, chunks, base),
        kinds,
        current,
        flags,
        gain,
        place,
        scale_hi,
        scale_lo,
        out_ref,
        wide,
        rows,
    )


def first_kernel(*refs):
    refs[-1][...] = jnp.zeros_like(refs[-1])


def opening_kernel(dims, flags, routes, gates, tokens, cotangent, gain, mark, *refs):
    peers, chunks = dims
    tables, out_ref, first, wide, rows = refs[:6], *refs[6:]
    make_tables(peers, routes, gates, *tables)
    current = choose([tokens, cotangent], 0, flags[2])
    first[...] = current
    dispatch_rows(
        (peers, chunks, 0), "FB", current, flags, gain, *tables[:3], out_ref, wide, rows
    )


def combine_kernel(dims, kinds, section_count, grad_count, has_final, flags, *refs):
    peers, chunks, base, grad_micro = dims
    returned = refs[0]
    sections = refs[1 : 1 + section_count]
    grads = refs[1 + section_count : 1 + section_count + grad_count]
    gain, pick, mix_hi, mix_lo = refs[1 + section_count + grad_count :][:4]
    out_ref, wide, rows = refs[-3:]
    is_forward, micro = flags[base], flags[base + 1]
    unpack(returned, rows, wide, peers, chunks)

    def forward():
        mixed = dot(mix_hi[micro], rows[...]) + dot(mix_lo[micro], rows[...])
        out_ref[...] = (choose(sections, 0, flags[base + 2]).astype(F32) + mixed).astype(BF16)

    def backward():
        section_in = choose(sections, 0, flags[base + 2]).astype(F32)
        grad_next = choose(grads, grad_micro, flags[base + 3]).astype(F32)
        inverse = lax.rsqrt(jnp.mean(section_in * section_in, axis=-1, keepdims=True) + EPS)
        scaled = dot(pick[micro], rows[...]) * gain[...]
        normed = section_in * inverse
        shared = jnp.mean(scaled * normed, axis=-1, keepdims=True)
        result = (grad_next + inverse * (scaled - normed * shared)).astype(BF16)
        if has_final:
            final = refs[-4]
            out_ref[...] = final[...]

            @pl.when(flags[base + 2 - 6] == 1)
            def _():
                out_ref[1] = result

        else:
            out_ref[...] = result

    if kinds == "F":
        forward()
    elif kinds == "B":
        backward()
    else:
        pl.when(is_forward == 1)(forward)
        pl.when(is_forward == 0)(backward)


def assemble_kernel(flags, *refs):
    mixed, (hidden, input_grads) = refs[:-2], refs[-2:]
    for micro in range(hidden.shape[0]):
        kept = [mixed[micro], mixed[1 + micro], mixed[2 + micro], mixed[5 + micro]]
        hidden[micro] = choose(kept, 0, flags[3])
        kept = [mixed[min(6, 6 + micro - rank)] for rank in range(4)]
        input_grads[micro] = choose(kept, 0, flags[3])


def sum_kernel(*refs):
    count = len(refs) // 3
    for own, other, out in zip(refs[:count], refs[count : 2 * count], refs[2 * count :]):
        out[...] = own[...].astype(F32) + other[...].astype(F32)


def forward_kernel(
    dims, has_store, received, w_gate, w_up, w_down, in_a, in_b, down_a, down_b, *refs
):
    peers, chunks, low_rank, block, slot = dims
    sent, rows, low_in, gate_pre, up_pre, wide, acts = refs[4 * has_store :]
    slots = rows.shape[1]
    unpack(received, rows.at[slot], wide, peers, chunks)
    slot_rows = rows[slot]
    low = dot_nt(slot_rows, in_a[...]).astype(BF16)
    low_in[slot] = low
    low_total = jnp.zeros((slots, low_rank), F32)
    for start in range(0, w_gate.shape[1], block):
        piece = pl.ds(start, block)
        gate = dot(slot_rows, w_gate[:, piece]) + dot(low[:, :low_rank], in_b[0, :, piece])
        up = dot(slot_rows, w_up[:, piece]) + dot(low[:, low_rank:], in_b[1, :, piece])
        gate_pre[slot, :, piece] = gate
        up_pre[slot, :, piece] = up
        activated = (gate * jax.nn.sigmoid(gate) * up).astype(BF16)
        low_total += dot_nt(activated, down_a[:, piece])
        acts[:, piece] = activated
    low_down = low_total.astype(BF16)
    pack(
        lambda start, size: dot(acts[...], w_down[:, start : start + size])
        + dot(low_down, down_b[:, start : start + size]),
        sent,
        wide,
        peers,
        chunks,
    )


def backward_kernel(dims, received_count, has_other, has_totals, is_last, flags, *refs):
    peers, chunks, low_rank, block, base = dims
    received = refs[:received_count]
    other = refs[received_count]
    refs = refs[received_count + has_other + 4 * has_totals :]
    (rows, low_in, gate_pre, up_pre, w_gate, w_up, w_down, in_a, in_b, down_a, down_b) = refs[:11]
    (sent, grad_in_a, grad_in_b, grad_down_a, grad_down_b) = refs[11:16]
    (wide, grad_out, total) = refs[-3:]
    active, slot = flags[base] == 1, flags[base + 1]
    slots = rows.shape[1]

    def store(ref, where, value):
        ref[where] = jnp.where(flags[base + 3] == 1, ref[where] + value, value) if has_totals else value

    @pl.when(active)
    def _():
        if received_count == 1:
            unpack(received[0], grad_out, wide, peers, chunks)
        else:
            for index in range(received_count):

                @pl.when(flags[base + 2] == index)
                def _():
                    unpack(received[index], grad_out, wide, peers, chunks)

        grad = grad_out[...]
        grad_low_down = dot_nt(grad, down_b[...]).astype(BF16)
        low = low_in[slot]
        low_total = jnp.zeros((slots, low_rank), F32)
        gate_low = jnp.zeros((slots, low_rank), F32)
        up_low = jnp.zeros((slots, low_rank), F32)
        for start in range(0, w_gate.shape[1], block):
            piece = pl.ds(start, block)
            gate, up = gate_pre[slot, :, piece], up_pre[slot, :, piece]
            sigmoid = jax.nn.sigmoid(gate)
            silu = gate * sigmoid
            activated = (silu * up).astype(BF16)
            grad_act = dot_nt(grad, w_down[piece, :]) + dot(grad_low_down, down_a[:, piece])
            grad_gate = (grad_act * up * sigmoid * (1.0 + gate * (1.0 - sigmoid))).astype(BF16)
            grad_up = (grad_act * silu).astype(BF16)
            store(grad_in_b, (0, slice(None), piece), dot_tn(low[:, :low_rank], grad_gate))
            store(grad_in_b, (1, slice(None), piece), dot_tn(low[:, low_rank:], grad_up))
            store(grad_down_a, (slice(None), piece), dot_tn(grad_low_down, activated))
            low_total += dot_nt(activated, down_a[:, piece])
            gate_low += dot_nt(grad_gate, in_b[0, :, piece])
            up_low += dot_nt(grad_up, in_b[1, :, piece])
            part = dot_nt(grad_gate, w_gate[:, piece]) + dot_nt(grad_up, w_up[:, piece])
            total[...] = part if start == 0 else total[...] + part
        low_grad = jnp.concatenate([gate_low, up_low], axis=1).astype(BF16)
        pack(
            lambda start, size: total[:, start : start + size]
            + dot(low_grad, in_a[:, start : start + size]),
            sent,
            wide,
            peers,
            chunks,
        )
        store(grad_in_a, ..., dot_tn(low_grad, rows[slot]))
        store(grad_down_b, ..., dot_tn(low_total.astype(BF16), grad))

    if has_other:

        @pl.when(jnp.logical_not(active))
        def _():
            sent[...] = other[...]

    if is_last:
        for total, rounded in zip(refs[12:16], refs[16:20]):
            rounded[...] = total[...].astype(BF16)


def params(megabytes):
    return pltpu.CompilerParams(vmem_limit_bytes=megabytes * 1024 * 1024)


def rank_flags(sections, micros):
    assert sections == 4 and micros == 2
    last = sections - 1
    ticks = 2 * sections
    table = np.zeros((sections, ticks, 12), np.int32)
    for rank in range(sections):
        for tick in range(ticks):
            row = table[rank, tick]
            row[3] = rank
            forward = tick - rank if tick - rank in (0, 1) else None
            backward = tick - (2 * last - rank)
            backward = backward if backward in (0, 1) else None
            if forward is not None:
                row[0:2] = 1, forward
            elif backward is not None:
                row[0:2] = 0, backward
            elif rank == last and tick < 2:
                row[0:2] = 0, tick
            if tick == 0:
                row[2] = 1 if rank == last else 0
            elif tick == 1:
                row[2] = 2 if rank == last else (0 if rank == 0 else 1)
            if backward is not None:
                row[4:6] = 1, rank + backward
                row[6] = 0 if rank == last else 1
                row[7] = backward
                row[8:10] = 0, backward
            elif forward is not None:
                row[8:10] = 1, forward
            elif rank == last and tick in (5, 6):
                row[8:10] = 1, tick - 5
            if tick == 4:
                row[10:12] = (0, 0) if rank == last else (1, 1)
            elif tick == 5:
                row[10] = 1 if rank == 1 else 0
            elif tick == 6:
                row[10] = {1: 0, 0: 1, 3: 2}.get(rank, 0)
    return table.reshape(sections, -1)


def body(
    tokens, cotangent, routes, gates, norm_gain, w_gate, w_up, w_down, in_a, in_b, down_a, down_b
):
    section_index = lax.axis_index("pipe")
    sections = lax.axis_size("pipe")
    peers = lax.axis_size("expert")
    micros, tok_rows, model = tokens.shape
    hidden_width = w_gate.shape[3]
    low_rank = down_a.shape[3]
    slots = SLOTS * peers
    chunks = model // LANES
    ticks = 2 * sections
    forward_ticks = sections + micros - 1
    block = hidden_width // 3
    flags = lax.dynamic_index_in_dim(
        jnp.asarray(rank_flags(sections, micros)), section_index, 0, keepdims=False
    )
    w_gate, w_up, w_down = w_gate[0, 0], w_up[0, 0], w_down[0, 0]
    in_a, in_b, down_a, down_b = in_a[0, 0].T, in_b[0, 0], down_a[0, 0].T, down_b[0, 0]
    buffer = jax.ShapeDtypeStruct((peers, SLOTS * chunks, LANES), BF16)
    block_rows = jax.ShapeDtypeStruct((tok_rows, model), BF16)
    wide = pltpu.VMEM((peers * SLOTS * chunks, LANES), F32)

    routes, gates = routes[0], gates[0]
    held = pl.BlockSpec(memory_space=pltpu.VMEM)
    scalars = pl.BlockSpec(memory_space=pltpu.SMEM)
    table_in = jax.ShapeDtypeStruct((micros, slots, tok_rows), BF16)
    table_out = jax.ShapeDtypeStruct((micros, tok_rows, slots), BF16)
    weights = (w_gate, w_up, w_down, in_a, in_b, down_a, down_b)
    mark = pl.pallas_call(
        first_kernel,
        out_shape=jax.ShapeDtypeStruct((8, LANES), F32),
        in_specs=[pl.BlockSpec(memory_space=pl.ANY)] * (len(weights) + 3),
        out_specs=held,
        compiler_params=params(60),
        name="first",
    )(*weights, tokens, cotangent, norm_gain)
    *tables, placed_first, input_first = pl.pallas_call(
        functools.partial(opening_kernel, (peers, chunks)),
        out_shape=[table_in] * 3 + [table_out] * 3 + [buffer, block_rows],
        in_specs=[scalars] + [held] * 6,
        out_specs=[held] * 8,
        scratch_shapes=[wide, pltpu.VMEM((tok_rows, model), BF16)],
        compiler_params=params(10),
        name="opening",
    )(flags, routes.transpose(0, 2, 1), gates.transpose(0, 2, 1), tokens, cotangent, norm_gain, mark)
    place, scale_hi, scale_lo, pick, mix_hi, mix_lo = tables

    def exchange(rows):
        return lax.all_to_all(rows, "expert", split_axis=0, concat_axis=0, tiled=True)

    def dispatch(tick, kinds, sources):
        single = len(sources) == 1
        operands = [*sources, norm_gain, place, scale_hi, scale_lo]
        result = pl.pallas_call(
            functools.partial(
                dispatch_kernel, (peers, chunks, tick * 12, tick), kinds, len(sources)
            ),
            out_shape=[buffer] if single else [buffer, block_rows],
            in_specs=[scalars] + [held] * len(operands),
            out_specs=[held] * (1 if single else 2),
            scratch_shapes=[wide, pltpu.VMEM((tok_rows, model), BF16)],
            compiler_params=params(20),
            name="dispatch",
        )(flags, *operands)
        return result[0], sources[0] if single else result[1]

    def combine(tick, kinds, returned, section_inputs, grads, final):
        finals = [] if final is None else [final]
        operands = [returned, *section_inputs, *grads, norm_gain, pick, mix_hi, mix_lo, *finals]
        return pl.pallas_call(
            functools.partial(
                combine_kernel,
                (peers, chunks, tick * 12 + 8, tick - sections + 1),
                kinds,
                len(section_inputs),
                len(grads),
                len(finals) > 0,
            ),
            out_shape=block_rows if final is None else jax.ShapeDtypeStruct(final.shape, BF16),
            in_specs=[scalars] + [held] * len(operands),
            out_specs=held,
            input_output_aliases={len(operands): 0} if finals else {},
            scratch_shapes=[wide, pltpu.VMEM((slots, model), BF16)],
            compiler_params=params(20),
            name="combine",
        )(flags, *operands)

    state_shapes = [
        jax.ShapeDtypeStruct((forward_ticks, slots, model), BF16),
        jax.ShapeDtypeStruct((forward_ticks, slots, 2 * low_rank), BF16),
        jax.ShapeDtypeStruct((forward_ticks, slots, hidden_width), F32),
        jax.ShapeDtypeStruct((forward_ticks, slots, hidden_width), F32),
    ]

    def expert_forward(tick, received, state):
        has_store = state is not None
        result = pl.pallas_call(
            functools.partial(forward_kernel, (peers, chunks, low_rank, block, tick), has_store),
            out_shape=[buffer] + state_shapes,
            in_specs=[held] * (12 if has_store else 8),
            out_specs=[held] * 5,
            scratch_shapes=[wide, pltpu.VMEM((slots, hidden_width), BF16)],
            input_output_aliases={8: 1, 9: 2, 10: 3, 11: 4} if has_store else {},
            compiler_params=params(20),
            name="expert_forward",
        )(received, *weights, *(state if has_store else ()))
        return result[0], result[1:]

    def expert_backward(tick, received, other, state, totals):
        base = tick * 12 + 4
        others = [] if other is None else [other]
        operands = [*received, *others, *totals, *state, *weights]
        first = 1 + len(received) + len(others)
        is_last = tick == ticks - 1
        sums = [
            (2 * low_rank, model),
            (2, low_rank, hidden_width),
            (low_rank, hidden_width),
            (low_rank, model),
        ]
        return pl.pallas_call(
            functools.partial(
                backward_kernel,
                (peers, chunks, low_rank, block, base),
                len(received),
                len(others),
                len(totals) > 0,
                is_last,
            ),
            out_shape=[buffer]
            + [jax.ShapeDtypeStruct(shape, F32) for shape in sums]
            + [jax.ShapeDtypeStruct(shape, BF16) for shape in sums * is_last],
            in_specs=[scalars] + [held] * len(operands),
            out_specs=[held] * (9 if is_last else 5),
            input_output_aliases={first + item: 1 + item for item in range(len(totals))},
            scratch_shapes=[
                wide,
                pltpu.VMEM((slots, model), BF16),
                pltpu.VMEM((slots, model), F32),
            ],
            compiler_params=params(20),
            name="expert_backward",
        )(flags, *operands)

    hops = [
        [(0, 1)],
        [(1, 2), (0, 1)],
        [(2, 3), (1, 2)],
        [(2, 3), (3, 2)],
        [(2, 1), (3, 2)],
        [(1, 0), (2, 1)],
        [(1, 0)],
    ]
    inputs, got, sent, mixed = {}, {}, {}, {}
    state, totals = None, ()
    for tick in range(ticks):
        if tick == 1:
            sources = [tokens, incoming, cotangent]
        elif tick > 1:
            sources = [incoming]
        kinds = {1: "FB", 2: "F", 3: "F", 4: "FB"}.get(tick, "B")
        if tick == 0:
            placed, inputs[tick] = placed_first, input_first
        else:
            placed, inputs[tick] = dispatch(tick, kinds, sources)
        got[tick] = exchange(placed)
        if tick < forward_ticks:
            sent[tick], state = expert_forward(tick, got[tick], state)
            answer = sent[tick]
        if tick >= 3:
            received = [got[index] for index in {3: (0,), 4: (1, 4)}.get(tick, (tick,))]
            other = sent[{3: 3, 5: 3, 6: 4}[tick]] if tick in (3, 5, 6) else None
            answer, *totals = expert_backward(tick, received, other, state, totals)
        returned = exchange(answer)
        if tick == ticks - 1:
            returned, rounded = lax.optimization_barrier((returned, totals[4:]))
        section_inputs = {4: (4, 2), 5: (3, 1), 6: (2, 0, 4), 7: (1,)}.get(tick, (tick,))
        grads = {3: [cotangent], 4: [cotangent, inputs[tick]]}.get(
            tick, [inputs[tick]] if tick > 4 else []
        )
        kinds = "F" if tick < 3 else "B" if tick in (4, 7) else "FB"
        final = input_grads if tick == ticks - 1 else None
        mixed[tick] = combine(
            tick, kinds, returned, [inputs[index] for index in section_inputs], grads, final
        )
        if tick < ticks - 1:
            incoming = lax.ppermute(mixed[tick], "pipe", hops[tick])
        if tick == ticks - 2:
            pair = jax.ShapeDtypeStruct((micros, tok_rows, model), BF16)
            hidden, input_grads = pl.pallas_call(
                assemble_kernel,
                out_shape=[pair] * 2,
                in_specs=[scalars] + [held] * (ticks - 1),
                out_specs=[held] * 2,
                compiler_params=params(8),
                name="assemble",
            )(flags, *[mixed[index] for index in range(ticks - 1)])
            incoming, hidden, input_grads = lax.optimization_barrier(
                (incoming, hidden, input_grads)
            )

    input_grads = mixed[ticks - 1]

    across = [lax.ppermute(total, "dp", [(0, 1), (1, 0)]) for total in rounded]
    totals = pl.pallas_call(
        sum_kernel,
        out_shape=[jax.ShapeDtypeStruct(total.shape, F32) for total in rounded],
        in_specs=[held] * (2 * len(rounded)),
        out_specs=[held] * len(rounded),
        compiler_params=params(8),
        name="sums",
    )(*rounded, *across)
    return (
        hidden[None],
        input_grads[None],
        totals[0].T[None, None],
        totals[1][None, None],
        totals[2].T[None, None],
        totals[3][None, None],
    )


def solution(mesh):
    placed = (
        P(None, ("expert", "dp"), None),
        P(None, ("expert", "dp"), None),
        P("pipe", None, ("expert", "dp"), None),
        P("pipe", None, ("expert", "dp"), None),
        P("pipe", None),
        P("pipe", "expert", None, None),
        P("pipe", "expert", None, None),
        P("pipe", "expert", None, None),
        P("pipe", "expert", None, None),
        P("pipe", "expert", None, None, None),
        P("pipe", "expert", None, None),
        P("pipe", "expert", None, None),
    )
    return jax.shard_map(
        body,
        mesh=mesh,
        in_specs=placed,
        out_specs=(
            P("pipe", None, ("expert", "dp"), None),
            P("pipe", None, ("expert", "dp"), None),
            P("pipe", "expert", None, None),
            P("pipe", "expert", None, None, None),
            P("pipe", "expert", None, None),
            P("pipe", "expert", None, None),
        ),
        check_vma=False,
    )
```

```python
import functools

import jax
import jax.numpy as jnp
import numpy as np
from jax import lax
from jax.experimental import pallas as pl
from jax.experimental.pallas import tpu as pltpu
from jax.sharding import PartitionSpec as P

EPS = 1e-06
SLOTS = 6
LANES = 128
F32 = jnp.float32
BF16 = jnp.bfloat16


def dot(left, right):
    return jnp.dot(left, right, preferred_element_type=F32)


def dot_nt(left, right):
    return lax.dot_general(left, right, (((1,), (1,)), ((), ())), preferred_element_type=F32)


def dot_tn(left, right):
    return lax.dot_general(left, right, (((0,), (0,)), ((), ())), preferred_element_type=F32)


def pack(columns, out_ref, wide, peers, chunks):
    stride = SLOTS * chunks
    step = 4
    for first in range(0, chunks, step):
        block = columns(first * LANES, step * LANES)
        for slot in range(SLOTS):
            for chunk in range(step):
                wide[pl.ds(slot * chunks + first + chunk, peers, stride=stride), :] = block[
                    slot * peers : (slot + 1) * peers, chunk * LANES : (chunk + 1) * LANES
                ]
    for peer in range(peers):
        out_ref[peer] = wide[peer * stride : (peer + 1) * stride, :].astype(BF16)


def unpack(in_ref, rows, wide, peers, chunks):
    stride = SLOTS * chunks
    for peer in range(peers):
        wide[peer * stride : (peer + 1) * stride, :] = in_ref[peer].astype(F32)
    for slot in range(SLOTS):
        for chunk in range(chunks):
            rows[slot * peers : (slot + 1) * peers, chunk * LANES : (chunk + 1) * LANES] = wide[
                pl.ds(slot * chunks + chunk, peers, stride=stride), :
            ].astype(BF16)


def split(weight):
    high = weight.astype(BF16)
    return high, (weight - high.astype(F32)).astype(BF16)


def make_tables(peers, routes, gates, place, scale_hi, scale_lo, pick, mix_hi, mix_lo):
    micros, _, rows = routes.shape
    slots = SLOTS * peers
    assert peers & (peers - 1) == 0
    number = lax.broadcasted_iota(jnp.int32, (slots, rows), 0)
    expert, position = number & (peers - 1), (number >> (peers.bit_length() - 1)).astype(F32)
    down = lax.broadcasted_iota(jnp.int32, (rows, rows), 0)
    across = lax.broadcasted_iota(jnp.int32, (rows, rows), 1)
    earlier = jnp.where(down < across, 1.0, 0.0).astype(BF16)
    for micro in range(micros):
        first = routes[micro, 0:1, :] == expert
        second = routes[micro, 1:2, :] == expert
        named = jnp.where(first | second, 1.0, 0.0)
        before = dot(named.astype(BF16), earlier)
        chosen = jnp.where(before == position, named, 0.0)
        weight = chosen * (
            jnp.where(first, gates[micro, 0:1, :], 0.0) + jnp.where(second, gates[micro, 1:2, :], 0.0)
        )
        place[micro] = chosen.astype(BF16)
        scale_hi[micro], scale_lo[micro] = split(weight)
        pick[micro] = chosen.T.astype(BF16)
        mix_hi[micro], mix_lo[micro] = split(weight.T)


def choose(refs, micro, which):
    blocks = [ref[...] if len(ref.shape) == 2 else ref[micro] for ref in refs]
    value = blocks[0]
    for index in range(1, len(blocks)):
        value = jnp.where(which == index, blocks[index], value)
    return value


def dispatch_rows(dims, kinds, current, flags, gain, place, scale_hi, scale_lo, out_ref, wide, rows):
    peers, chunks, base = dims
    is_forward, micro = flags[base], flags[base + 1]

    def forward():
        values = current.astype(F32)
        inverse = lax.rsqrt(jnp.mean(values * values, axis=-1, keepdims=True) + EPS)
        rows[...] = (values * inverse * gain[...]).astype(BF16)
        pack(
            lambda start, size: dot(place[micro], rows[:, start : start + size]),
            out_ref,
            wide,
            peers,
            chunks,
        )

    def backward():
        rows[...] = current
        pack(
            lambda start, size: dot(scale_hi[micro], rows[:, start : start + size])
            + dot(scale_lo[micro], rows[:, start : start + size]),
            out_ref,
            wide,
            peers,
            chunks,
        )

    if kinds == "F":
        forward()
    elif kinds == "B":
        backward()
    else:
        pl.when(is_forward == 1)(forward)
        pl.when(is_forward == 0)(backward)


def dispatch_kernel(dims, kinds, source_count, flags, *refs):
    peers, chunks, base, tick = dims
    sources = refs[:source_count]
    gain, place, scale_hi, scale_lo, out_ref = refs[source_count : source_count + 5]
    wide, rows = refs[-2:]
    current = choose(sources, tick, flags[base + 2])
    if source_count > 1:
        refs[source_count + 5][...] = current
    dispatch_rows(
        (peers, chunks, base),
        kinds,
        current,
        flags,
        gain,
        place,
        scale_hi,
        scale_lo,
        out_ref,
        wide,
        rows,
    )


def first_kernel(*refs):
    refs[-1][...] = jnp.zeros_like(refs[-1])


def opening_kernel(dims, flags, routes, gates, tokens, cotangent, gain, mark, *refs):
    peers, chunks = dims
    tables, out_ref, first, wide, rows = refs[:6], *refs[6:]
    make_tables(peers, routes, gates, *tables)
    current = choose([tokens, cotangent], 0, flags[2])
    first[...] = current
    dispatch_rows(
        (peers, chunks, 0), "FB", current, flags, gain, *tables[:3], out_ref, wide, rows
    )


def combine_kernel(dims, kinds, section_count, grad_count, has_final, flags, *refs):
    peers, chunks, base, grad_micro = dims
    returned = refs[0]
    sections = refs[1 : 1 + section_count]
    grads = refs[1 + section_count : 1 + section_count + grad_count]
    gain, pick, mix_hi, mix_lo = refs[1 + section_count + grad_count :][:4]
    out_ref, wide, rows = refs[-3:]
    is_forward, micro = flags[base], flags[base + 1]
    unpack(returned, rows, wide, peers, chunks)

    def forward():
        mixed = dot(mix_hi[micro], rows[...]) + dot(mix_lo[micro], rows[...])
        out_ref[...] = (choose(sections, 0, flags[base + 2]).astype(F32) + mixed).astype(BF16)

    def backward():
        section_in = choose(sections, 0, flags[base + 2]).astype(F32)
        grad_next = choose(grads, grad_micro, flags[base + 3]).astype(F32)
        inverse = lax.rsqrt(jnp.mean(section_in * section_in, axis=-1, keepdims=True) + EPS)
        scaled = dot(pick[micro], rows[...]) * gain[...]
        normed = section_in * inverse
        shared = jnp.mean(scaled * normed, axis=-1, keepdims=True)
        result = (grad_next + inverse * (scaled - normed * shared)).astype(BF16)
        if has_final:
            final = refs[-4]
            out_ref[...] = final[...]

            @pl.when(flags[base + 2 - 6] == 1)
            def _():
                out_ref[1] = result

        else:
            out_ref[...] = result

    if kinds == "F":
        forward()
    elif kinds == "B":
        backward()
    else:
        pl.when(is_forward == 1)(forward)
        pl.when(is_forward == 0)(backward)


def assemble_kernel(flags, *refs):
    mixed, (hidden, input_grads) = refs[:-2], refs[-2:]
    for micro in range(hidden.shape[0]):
        kept = [mixed[micro], mixed[1 + micro], mixed[2 + micro], mixed[5 + micro]]
        hidden[micro] = choose(kept, 0, flags[3])
        kept = [mixed[min(6, 6 + micro - rank)] for rank in range(4)]
        input_grads[micro] = choose(kept, 0, flags[3])


def sum_kernel(*refs):
    count = len(refs) // 3
    for own, other, out in zip(refs[:count], refs[count : 2 * count], refs[2 * count :]):
        out[...] = own[...].astype(F32) + other[...].astype(F32)


def forward_kernel(
    dims, has_store, received, w_gate, w_up, w_down, in_a, in_b, down_a, down_b, *refs
):
    peers, chunks, low_rank, block, slot = dims
    sent, rows, low_in, gate_pre, up_pre, wide, acts = refs[4 * has_store :]
    slots = rows.shape[1]
    unpack(received, rows.at[slot], wide, peers, chunks)
    slot_rows = rows[slot]
    low = dot_nt(slot_rows, in_a[...]).astype(BF16)
    low_in[slot] = low
    low_total = jnp.zeros((slots, low_rank), F32)
    for start in range(0, w_gate.shape[1], block):
        piece = pl.ds(start, block)
        gate = dot(slot_rows, w_gate[:, piece]) + dot(low[:, :low_rank], in_b[0, :, piece])
        up = dot(slot_rows, w_up[:, piece]) + dot(low[:, low_rank:], in_b[1, :, piece])
        gate_pre[slot, :, piece] = gate
        up_pre[slot, :, piece] = up
        activated = (gate * jax.nn.sigmoid(gate) * up).astype(BF16)
        low_total += dot_nt(activated, down_a[:, piece])
        acts[:, piece] = activated
    low_down = low_total.astype(BF16)
    pack(
        lambda start, size: dot(acts[...], w_down[:, start : start + size])
        + dot(low_down, down_b[:, start : start + size]),
        sent,
        wide,
        peers,
        chunks,
    )


def backward_kernel(dims, received_count, has_other, has_totals, is_last, flags, *refs):
    peers, chunks, low_rank, block, base = dims
    received = refs[:received_count]
    other = refs[received_count]
    refs = refs[received_count + has_other + 4 * has_totals :]
    (rows, low_in, gate_pre, up_pre, w_gate, w_up, w_down, in_a, in_b, down_a, down_b) = refs[:11]
    (sent, grad_in_a, grad_in_b, grad_down_a, grad_down_b) = refs[11:16]
    (wide, grad_out, total) = refs[-3:]
    active, slot = flags[base] == 1, flags[base + 1]
    slots = rows.shape[1]

    def store(ref, where, value):
        ref[where] = jnp.where(flags[base + 3] == 1, ref[where] + value, value) if has_totals else value

    @pl.when(active)
    def _():
        if received_count == 1:
            unpack(received[0], grad_out, wide, peers, chunks)
        else:
            for index in range(received_count):

                @pl.when(flags[base + 2] == index)
                def _():
                    unpack(received[index], grad_out, wide, peers, chunks)

        grad = grad_out[...]
        grad_low_down = dot_nt(grad, down_b[...]).astype(BF16)
        low = low_in[slot]
        low_total = jnp.zeros((slots, low_rank), F32)
        gate_low = jnp.zeros((slots, low_rank), F32)
        up_low = jnp.zeros((slots, low_rank), F32)
        for start in range(0, w_gate.shape[1], block):
            piece = pl.ds(start, block)
            gate, up = gate_pre[slot, :, piece], up_pre[slot, :, piece]
            sigmoid = jax.nn.sigmoid(gate)
            silu = gate * sigmoid
            activated = (silu * up).astype(BF16)
            grad_act = dot_nt(grad, w_down[piece, :]) + dot(grad_low_down, down_a[:, piece])
            grad_gate = (grad_act * up * sigmoid * (1.0 + gate * (1.0 - sigmoid))).astype(BF16)
            grad_up = (grad_act * silu).astype(BF16)
            store(grad_in_b, (0, slice(None), piece), dot_tn(low[:, :low_rank], grad_gate))
            store(grad_in_b, (1, slice(None), piece), dot_tn(low[:, low_rank:], grad_up))
            store(grad_down_a, (slice(None), piece), dot_tn(grad_low_down, activated))
            low_total += dot_nt(activated, down_a[:, piece])
            gate_low += dot_nt(grad_gate, in_b[0, :, piece])
            up_low += dot_nt(grad_up, in_b[1, :, piece])
            part = dot_nt(grad_gate, w_gate[:, piece]) + dot_nt(grad_up, w_up[:, piece])
            total[...] = part if start == 0 else total[...] + part
        low_grad = jnp.concatenate([gate_low, up_low], axis=1).astype(BF16)
        pack(
            lambda start, size: total[:, start : start + size]
            + dot(low_grad, in_a[:, start : start + size]),
            sent,
            wide,
            peers,
            chunks,
        )
        store(grad_in_a, ..., dot_tn(low_grad, rows[slot]))
        store(grad_down_b, ..., dot_tn(low_total.astype(BF16), grad))

    if has_other:

        @pl.when(jnp.logical_not(active))
        def _():
            sent[...] = other[...]

    if is_last:
        for total, rounded in zip(refs[12:16], refs[16:20]):
            rounded[...] = total[...].astype(BF16)


def params(megabytes):
    return pltpu.CompilerParams(vmem_limit_bytes=megabytes * 1024 * 1024)


def rank_flags(sections, micros):
    assert sections == 4 and micros == 2
    last = sections - 1
    ticks = 2 * sections
    table = np.zeros((sections, ticks, 12), np.int32)
    for rank in range(sections):
        for tick in range(ticks):
            row = table[rank, tick]
            row[3] = rank
            forward = tick - rank if tick - rank in (0, 1) else None
            backward = tick - (2 * last - rank)
            backward = backward if backward in (0, 1) else None
            if forward is not None:
                row[0:2] = 1, forward
            elif backward is not None:
                row[0:2] = 0, backward
            elif rank == last and tick < 2:
                row[0:2] = 0, tick
            if tick == 0:
                row[2] = 1 if rank == last else 0
            elif tick == 1:
                row[2] = 2 if rank == last else (0 if rank == 0 else 1)
            if backward is not None:
                row[4:6] = 1, rank + backward
                row[6] = 0 if rank == last else 1
                row[7] = backward
                row[8:10] = 0, backward
            elif forward is not None:
                row[8:10] = 1, forward
            elif rank == last and tick in (5, 6):
                row[8:10] = 1, tick - 5
            if tick == 4:
                row[10:12] = (0, 0) if rank == last else (1, 1)
            elif tick == 5:
                row[10] = 1 if rank == 1 else 0
            elif tick == 6:
                row[10] = {1: 0, 0: 1, 3: 2}.get(rank, 0)
    return table.reshape(sections, -1)


def body(
    tokens, cotangent, routes, gates, norm_gain, w_gate, w_up, w_down, in_a, in_b, down_a, down_b
):
    section_index = lax.axis_index("pipe")
    sections = lax.axis_size("pipe")
    peers = lax.axis_size("expert")
    micros, tok_rows, model = tokens.shape
    hidden_width = w_gate.shape[3]
    low_rank = down_a.shape[3]
    slots = SLOTS * peers
    chunks = model // LANES
    ticks = 2 * sections
    forward_ticks = sections + micros - 1
    block = hidden_width // 3
    flags = lax.dynamic_index_in_dim(
        jnp.asarray(rank_flags(sections, micros)), section_index, 0, keepdims=False
    )
    w_gate, w_up, w_down = w_gate[0, 0], w_up[0, 0], w_down[0, 0]
    in_a, in_b, down_a, down_b = in_a[0, 0].T, in_b[0, 0], down_a[0, 0].T, down_b[0, 0]
    buffer = jax.ShapeDtypeStruct((peers, SLOTS * chunks, LANES), BF16)
    block_rows = jax.ShapeDtypeStruct((tok_rows, model), BF16)
    wide = pltpu.VMEM((peers * SLOTS * chunks, LANES), F32)

    routes, gates = routes[0], gates[0]
    held = pl.BlockSpec(memory_space=pltpu.VMEM)
    scalars = pl.BlockSpec(memory_space=pltpu.SMEM)
    table_in = jax.ShapeDtypeStruct((micros, slots, tok_rows), BF16)
    table_out = jax.ShapeDtypeStruct((micros, tok_rows, slots), BF16)
    weights = (w_gate, w_up, w_down, in_a, in_b, down_a, down_b)
    mark = pl.pallas_call(
        first_kernel,
        out_shape=jax.ShapeDtypeStruct((8, LANES), F32),
        in_specs=[pl.BlockSpec(memory_space=pl.ANY)] * (len(weights) + 3),
        out_specs=held,
        compiler_params=params(60),
        name="first",
    )(*weights, tokens, cotangent, norm_gain)
    *tables, placed_first, input_first = pl.pallas_call(
        functools.partial(opening_kernel, (peers, chunks)),
        out_shape=[table_in] * 3 + [table_out] * 3 + [buffer, block_rows],
        in_specs=[scalars] + [held] * 6,
        out_specs=[held] * 8,
        scratch_shapes=[wide, pltpu.VMEM((tok_rows, model), BF16)],
        compiler_params=params(10),
        cost_estimate=pl.CostEstimate(flops=2 * 10**10, bytes_accessed=10**7, transcendentals=0),
        name="opening",
    )(flags, routes.transpose(0, 2, 1), gates.transpose(0, 2, 1), tokens, cotangent, norm_gain, mark)
    place, scale_hi, scale_lo, pick, mix_hi, mix_lo = tables

    def exchange(rows):
        return lax.all_to_all(rows, "expert", split_axis=0, concat_axis=0, tiled=True)

    def dispatch(tick, kinds, sources):
        single = len(sources) == 1
        operands = [*sources, norm_gain, place, scale_hi, scale_lo]
        result = pl.pallas_call(
            functools.partial(
                dispatch_kernel, (peers, chunks, tick * 12, tick), kinds, len(sources)
            ),
            out_shape=[buffer] if single else [buffer, block_rows],
            in_specs=[scalars] + [held] * len(operands),
            out_specs=[held] * (1 if single else 2),
            scratch_shapes=[wide, pltpu.VMEM((tok_rows, model), BF16)],
            compiler_params=params(20),
            name="dispatch",
        )(flags, *operands)
        return result[0], sources[0] if single else result[1]

    def combine(tick, kinds, returned, section_inputs, grads, final):
        finals = [] if final is None else [final]
        operands = [returned, *section_inputs, *grads, norm_gain, pick, mix_hi, mix_lo, *finals]
        return pl.pallas_call(
            functools.partial(
                combine_kernel,
                (peers, chunks, tick * 12 + 8, tick - sections + 1),
                kinds,
                len(section_inputs),
                len(grads),
                len(finals) > 0,
            ),
            out_shape=block_rows if final is None else jax.ShapeDtypeStruct(final.shape, BF16),
            in_specs=[scalars] + [held] * len(operands),
            out_specs=held,
            input_output_aliases={len(operands): 0} if finals else {},
            scratch_shapes=[wide, pltpu.VMEM((slots, model), BF16)],
            compiler_params=params(20),
            name="combine",
        )(flags, *operands)

    state_shapes = [
        jax.ShapeDtypeStruct((forward_ticks, slots, model), BF16),
        jax.ShapeDtypeStruct((forward_ticks, slots, 2 * low_rank), BF16),
        jax.ShapeDtypeStruct((forward_ticks, slots, hidden_width), F32),
        jax.ShapeDtypeStruct((forward_ticks, slots, hidden_width), F32),
    ]

    def expert_forward(tick, received, state):
        has_store = state is not None
        result = pl.pallas_call(
            functools.partial(
                forward_kernel, (peers, chunks, low_rank, hidden_width, tick), has_store
            ),
            out_shape=[buffer] + state_shapes,
            in_specs=[held] * (12 if has_store else 8),
            out_specs=[held] * 5,
            scratch_shapes=[wide, pltpu.VMEM((slots, hidden_width), BF16)],
            input_output_aliases={8: 1, 9: 2, 10: 3, 11: 4} if has_store else {},
            compiler_params=params(20),
            name="expert_forward",
        )(received, *weights, *(state if has_store else ()))
        return result[0], result[1:]

    def expert_backward(tick, received, other, state, totals):
        base = tick * 12 + 4
        others = [] if other is None else [other]
        operands = [*received, *others, *totals, *state, *weights]
        first = 1 + len(received) + len(others)
        is_last = tick == ticks - 1
        sums = [
            (2 * low_rank, model),
            (2, low_rank, hidden_width),
            (low_rank, hidden_width),
            (low_rank, model),
        ]
        return pl.pallas_call(
            functools.partial(
                backward_kernel,
                (peers, chunks, low_rank, block, base),
                len(received),
                len(others),
                len(totals) > 0,
                is_last,
            ),
            out_shape=[buffer]
            + [jax.ShapeDtypeStruct(shape, F32) for shape in sums]
            + [jax.ShapeDtypeStruct(shape, BF16) for shape in sums * is_last],
            in_specs=[scalars] + [held] * len(operands),
            out_specs=[held] * (9 if is_last else 5),
            input_output_aliases={first + item: 1 + item for item in range(len(totals))},
            scratch_shapes=[
                wide,
                pltpu.VMEM((slots, model), BF16),
                pltpu.VMEM((slots, model), F32),
            ],
            compiler_params=params(20),
            name="expert_backward",
        )(flags, *operands)

    hops = [
        [(0, 1)],
        [(1, 2), (0, 1)],
        [(2, 3), (1, 2)],
        [(2, 3), (3, 2)],
        [(2, 1), (3, 2)],
        [(1, 0), (2, 1)],
        [(1, 0)],
    ]
    inputs, got, sent, mixed = {}, {}, {}, {}
    state, totals = None, ()
    for tick in range(ticks):
        if tick == 1:
            sources = [tokens, incoming, cotangent]
        elif tick > 1:
            sources = [incoming]
        kinds = {1: "FB", 2: "F", 3: "F", 4: "FB"}.get(tick, "B")
        if tick == 0:
            placed, inputs[tick] = placed_first, input_first
        else:
            placed, inputs[tick] = dispatch(tick, kinds, sources)
        got[tick] = exchange(placed)
        if tick < forward_ticks:
            sent[tick], state = expert_forward(tick, got[tick], state)
            answer = sent[tick]
        if tick >= 3:
            received = [got[index] for index in {3: (0,), 4: (1, 4)}.get(tick, (tick,))]
            other = sent[{3: 3, 5: 3, 6: 4}[tick]] if tick in (3, 5, 6) else None
            answer, *totals = expert_backward(tick, received, other, state, totals)
        returned = exchange(answer)
        if tick == ticks - 1:
            returned, rounded = lax.optimization_barrier((returned, totals[4:]))
        section_inputs = {4: (4, 2), 5: (3, 1), 6: (2, 0, 4), 7: (1,)}.get(tick, (tick,))
        grads = {3: [cotangent], 4: [cotangent, inputs[tick]]}.get(
            tick, [inputs[tick]] if tick > 4 else []
        )
        kinds = "F" if tick < 3 else "B" if tick in (4, 7) else "FB"
        final = input_grads if tick == ticks - 1 else None
        mixed[tick] = combine(
            tick, kinds, returned, [inputs[index] for index in section_inputs], grads, final
        )
        if tick < ticks - 1:
            incoming = lax.ppermute(mixed[tick], "pipe", hops[tick])
        if tick == ticks - 2:
            pair = jax.ShapeDtypeStruct((micros, tok_rows, model), BF16)
            hidden, input_grads = pl.pallas_call(
                assemble_kernel,
                out_shape=[pair] * 2,
                in_specs=[scalars] + [held] * (ticks - 1),
                out_specs=[held] * 2,
                compiler_params=params(8),
                name="assemble",
            )(flags, *[mixed[index] for index in range(ticks - 1)])
            incoming, hidden, input_grads = lax.optimization_barrier(
                (incoming, hidden, input_grads)
            )

    input_grads = mixed[ticks - 1]

    across = [lax.ppermute(total, "dp", [(0, 1), (1, 0)]) for total in rounded]
    totals = pl.pallas_call(
        sum_kernel,
        out_shape=[jax.ShapeDtypeStruct(total.shape, F32) for total in rounded],
        in_specs=[held] * (2 * len(rounded)),
        out_specs=[held] * len(rounded),
        compiler_params=params(8),
        name="sums",
    )(*rounded, *across)
    return (
        hidden[None],
        input_grads[None],
        totals[0].T[None, None],
        totals[1][None, None],
        totals[2].T[None, None],
        totals[3][None, None],
    )


def solution(mesh):
    placed = (
        P(None, ("expert", "dp"), None),
        P(None, ("expert", "dp"), None),
        P("pipe", None, ("expert", "dp"), None),
        P("pipe", None, ("expert", "dp"), None),
        P("pipe", None),
        P("pipe", "expert", None, None),
        P("pipe", "expert", None, None),
        P("pipe", "expert", None, None),
        P("pipe", "expert", None, None),
        P("pipe", "expert", None, None, None),
        P("pipe", "expert", None, None),
        P("pipe", "expert", None, None),
    )
    return jax.shard_map(
        body,
        mesh=mesh,
        in_specs=placed,
        out_specs=(
            P("pipe", None, ("expert", "dp"), None),
            P("pipe", None, ("expert", "dp"), None),
            P("pipe", "expert", None, None),
            P("pipe", "expert", None, None, None),
            P("pipe", "expert", None, None),
            P("pipe", "expert", None, None),
        ),
        check_vma=False,
    )
```
